1024 devices in a mesh: gx: 8 (over y, core), gy: 8 (over z_hi, x), gz: 16 (over z_lo).
Axes of the slice: x: 4, y: 4, z: 32 (z_hi: 2, z_lo: 16; z = z_hi * 16 + z_lo), core: 2. Of those that a mesh axis runs over, the one named last changes fastest.
Arguments:
- node_feats: bfloat16 [8, 16, 32, 128, 128], P('gx', 'gy', 'gz'), may hold values from -6 to 6
- offsets: bfloat16 [8, 16, 32, 3, 128], P('gx', 'gy', 'gz'), may hold values from 0 to 1
- counts: int32 [8, 16, 32], P('gx', 'gy', 'gz'), may hold values from 0 to 128, as said below
- neighbours: int32 [8, 16, 32, 128, 8], P('gx', 'gy', 'gz'), may hold values from 0 to 3455, as said below
- pair_counts: int32 [8, 16, 32, 128], P('gx', 'gy', 'gz'), may hold values from 4 to 8
- radial_in: float32 [8, 64], replicated, may hold values from -2 to 2
- radial_out: bfloat16 [64, 384], replicated, may hold values from -0.75 to 0.75
- mix_weight: bfloat16 [512, 128], replicated, may hold values from -0.25 to 0.25
Outputs:
- updated: bfloat16 [8, 16, 32, 128, 128], P('gx', 'gy', 'gz')
The draws below stay inside these ranges and needn't reach their ends.
Inputs may be any that keep to these rules, and one draw needn't show every extreme that they name: `counts`: bins whose third index lies outside 32 // 4 to 23 are empty; the others hold at least 32 atoms, and some bin holds 128. `neighbours`: for an atom slot of a bin that holds atoms, every entry names an occupied slot of a bin that holds atoms among the 27 bins around it (digit 13 is the bin itself).
All inputs are finite; a program needn't handle non-finite values.
Results may differ from the reference program's by a relative error of at most 0.0081.
Values may be sent and summed in bfloat16 or wider, within the bound.
A program may use at most 32 MiB of HBM per device.

```python
import math
import jax
import jax.numpy as jnp
from jax import lax

C = 128
RADIAL = 64
BASIS = 8
SLOTS = 128
K = 8
NXB = 8
NYB = 16
NZB = 32


def bin_counts(key):
    key = jax.random.fold_in(key, 101)
    live_count = jax.random.randint(key, (NXB, NYB, NZB), SLOTS // 4, SLOTS + 1)
    layer_z = jnp.arange(NZB)[None, None, :]
    dense_layer = (layer_z >= NZB // 4) & (layer_z < NZB // 4 + NZB // 2)
    live_count = jnp.where(dense_layer, live_count, 0)
    live_count = live_count.at[0, 0, NZB // 4].set(SLOTS)
    live_count = live_count.at[1, 1, NZB // 4 + 1].set(SLOTS)
    return live_count.astype(jnp.int32)


def draw_counts(key, part):
    return bin_counts(key)


def draw_neighbours(key, part):
    live_count = bin_counts(key)
    key = jax.random.fold_in(key, 7)
    key_digit, key_slot = jax.random.split(key)
    full_shape = (NXB, NYB, NZB, SLOTS, K)
    bin_digit = jax.random.randint(key_digit, full_shape, 0, 27)
    grid_x = jnp.arange(NXB).reshape(NXB, 1, 1, 1, 1)
    grid_y = jnp.arange(NYB).reshape(1, NYB, 1, 1, 1)
    grid_z = jnp.arange(NZB).reshape(1, 1, NZB, 1, 1)
    there_x = (grid_x + bin_digit // 9 - 1) % NXB
    there_y = (grid_y + bin_digit // 3 % 3 - 1) % NYB
    there_z = (grid_z + bin_digit % 3 - 1) % NZB
    there_count = live_count[there_x, there_y, there_z]
    bin_digit = jnp.where(there_count > 0, bin_digit, 13)
    own_count = jnp.broadcast_to(live_count[:, :, :, None, None], full_shape)
    there_count = jnp.where(there_count > 0, there_count, own_count)
    slot_pick = jax.random.randint(key_slot, full_shape, 0, 1 << 20) % jnp.maximum(there_count, 1)
    chosen = bin_digit * SLOTS + slot_pick
    chosen = chosen.at[0, 0, NZB // 4, 0, 0].set(27 * SLOTS - 1)
    chosen = chosen.at[1, 1, NZB // 4 + 1, 0, 0].set(0)
    return chosen.astype(jnp.int32)


def draw_pair_counts(key, part):
    key = jax.random.fold_in(key, 9)
    chosen = jax.random.randint(key, (NXB, NYB, NZB, SLOTS), K // 2, K + 1)
    chosen = chosen.at[0, 0, 0, 0].set(K)
    chosen = chosen.at[0, 0, 0, 1].set(K // 2)
    return chosen.astype(jnp.int32)


def block_scale(own_key, extent, cuts, smallest, high):
    def one(dim, parts):
        heights = jax.random.uniform(jax.random.fold_in(jax.random.fold_in(own_key, 6), dim), (parts,), jnp.float32, smallest / len(cuts), high / len(cuts))
        return jnp.repeat(jnp.exp(heights), extent[dim] // parts).reshape((-1,) + (1,) * (len(extent) - dim - 1))

    factor_of = one(*cuts[0])
    for cut in cuts[1:]:
        factor_of = factor_of * one(*cut)
    return factor_of


def scatter_about(rng, extent, scale, bound, cuts=(), held_as=jnp.bfloat16):
    values = scale * jax.random.normal(rng, extent, jnp.float32)
    if cuts:
        values = values * block_scale(rng, extent, cuts, -0.22, 0.18)
    return jnp.clip(values, -bound, bound).astype(held_as)


def setup_inputs(seed: int = 0) -> dict:
    splits = jax.random.split(jax.random.key(seed), 9)
    node_feats = scatter_about(splits[0], (NXB, NYB, NZB, SLOTS, C), 1.0, 6.0, ((0, 8), (1, 8), (2, 16)))
    offsets = jnp.clip(1.0 * jax.random.uniform(splits[1], (NXB, NYB, NZB, 3, SLOTS), jnp.float32) ** block_scale(splits[1], (NXB, NYB, NZB, 3, SLOTS), ((0, 8), (1, 8), (2, 16)), -0.2, 0.2), 0.0, 1.0).astype(jnp.bfloat16)
    counts = draw_counts(jax.random.fold_in(splits[8], 71), 0)
    neighbours = draw_neighbours(jax.random.fold_in(splits[8], 71), 0)
    pair_counts = draw_pair_counts(jax.random.fold_in(splits[8], 71), 0)
    radial_in = scatter_about(splits[5], (BASIS, RADIAL), BASIS ** -0.5, 2.0, (), jnp.float32)
    radial_out = scatter_about(splits[6], (RADIAL, 3 * C), RADIAL ** -0.5, 0.75)
    mix_weight = scatter_about(splits[7], (4 * C, C), (4 * C) ** -0.5, 0.25)
    return dict(node_feats=node_feats, offsets=offsets, counts=counts, neighbours=neighbours, pair_counts=pair_counts, radial_in=radial_in, radial_out=radial_out, mix_weight=mix_weight)


ROOT_THREE = math.sqrt(3.0)
ROOT_FIVE = math.sqrt(5.0)
ROOT_FIFTEEN = math.sqrt(15.0)
CUTOFF_BINS = 3.0
FLOOR_BINS = 0.25

def bin_update(near_feats, near_offs, neighbour_rows, pair_count, atom_count, radial_in, radial_out, mix_weight):
    slot_total = near_feats.shape[3]
    channels = near_feats.shape[4]
    pair_width = neighbour_rows.shape[1]
    flat_index = neighbour_rows.reshape(-1)
    gathered = jnp.take(near_feats.reshape(27 * slot_total, channels), flat_index, axis=0)
    flat_offs = jnp.transpose(near_offs, (3, 0, 1, 2, 4)).reshape(3, 27 * slot_total).astype(jnp.float32)
    their_offs = jnp.take(flat_offs, flat_index, axis=1)
    own_offs = jnp.repeat(near_offs[1, 1, 1].astype(jnp.float32), pair_width, axis=1)
    bin_digit = flat_index // slot_total
    bin_shift = jnp.stack([bin_digit // 9 - 1, bin_digit // 3 % 3 - 1, bin_digit % 3 - 1]).astype(jnp.float32)
    displace = bin_shift + their_offs - own_offs
    distance = jnp.sqrt(lax.optimization_barrier(jnp.sum(displace * displace, axis=0)))
    floored = jnp.maximum(distance, FLOOR_BINS)
    scaled = jnp.minimum(distance / CUTOFF_BINS, 1.0)
    envelope = 1.0 - 10.0 * scaled ** 3 + 15.0 * scaled ** 4 - 6.0 * scaled ** 5
    orders = jnp.arange(1, radial_in.shape[0] + 1).astype(jnp.float32)[:, None]
    basis = jnp.sin(math.pi * orders * scaled[None, :]) * (envelope / floored)[None, :]
    hidden = jax.nn.silu(jnp.dot(radial_in.T, basis, precision=lax.Precision.HIGHEST)).astype(jnp.bfloat16)
    radial = lax.dot_general(hidden, radial_out, (((0,), (0,)), ((), ())), preferred_element_type=jnp.float32).astype(jnp.bfloat16)
    unit_vec = displace / floored[None, :]
    unit_x = unit_vec[0]
    unit_y = unit_vec[1]
    unit_z = unit_vec[2]
    harmonic = jnp.stack([jnp.ones_like(unit_x), ROOT_THREE * unit_x, ROOT_THREE * unit_y, ROOT_THREE * unit_z, ROOT_FIFTEEN * unit_x * unit_y, ROOT_FIFTEEN * unit_y * unit_z, ROOT_FIFTEEN * unit_z * unit_x, 0.5 * ROOT_FIVE * (3.0 * unit_z * unit_z - 1.0), 0.5 * ROOT_FIFTEEN * (unit_x * unit_x - unit_y * unit_y)])
    pair_mask = (jnp.arange(pair_width)[None, :] < pair_count[:, None]).astype(jnp.float32).reshape(-1)
    weighted = (harmonic * pair_mask[None, :] * pair_width ** (-0.5)).reshape(9, slot_total, pair_width)
    amp_list = []
    for order, (first_row, last_row) in enumerate(((0, 1), (1, 4), (4, 9))):
        product = radial[:, order * channels:(order + 1) * channels].astype(jnp.float32) * gathered.astype(jnp.float32)
        product = product.reshape(slot_total, pair_width, channels)
        comps = []
        for row in range(first_row, last_row):
            comps.append(lax.optimization_barrier(jnp.sum(weighted[row][:, :, None] * product, axis=1)))
        amp_list.append(jnp.stack(comps))
    scalar_part = amp_list[0][0].astype(jnp.bfloat16)
    vector_norm = lax.optimization_barrier(jnp.sum(amp_list[1] * amp_list[1], axis=0)).astype(jnp.bfloat16)
    tensor_norm = lax.optimization_barrier(jnp.sum(amp_list[2] * amp_list[2], axis=0)).astype(jnp.bfloat16)
    joined = jnp.concatenate([near_feats[1, 1, 1], scalar_part, vector_norm, tensor_norm], axis=1)
    mixed_rows = jnp.dot(joined, mix_weight, preferred_element_type=jnp.float32)
    live_slot = (jnp.arange(slot_total) < atom_count)[:, None]
    return jnp.where(live_slot, mixed_rows, 0.0).astype(jnp.bfloat16)

def reference(node_feats, offsets, counts, neighbours, pair_counts, radial_in, radial_out, mix_weight):
    margin = ((1, 1), (1, 1), (1, 1), (0, 0), (0, 0))
    padded_feats = jnp.pad(node_feats, margin, mode='wrap')
    padded_offs = jnp.pad(offsets, margin, mode='wrap')

    def update_one(bin_index):
        grid_x = (bin_index // (NYB * NZB)).astype(jnp.int32)
        grid_y = (bin_index // NZB % NYB).astype(jnp.int32)
        grid_z = (bin_index % NZB).astype(jnp.int32)
        anchor = jnp.zeros((), jnp.int32)
        near_feats = lax.dynamic_slice(padded_feats, (grid_x, grid_y, grid_z, anchor, anchor), (3, 3, 3, SLOTS, C))
        near_offs = lax.dynamic_slice(padded_offs, (grid_x, grid_y, grid_z, anchor, anchor), (3, 3, 3, 3, SLOTS))
        return bin_update(near_feats, near_offs, neighbours[grid_x, grid_y, grid_z], pair_counts[grid_x, grid_y, grid_z], counts[grid_x, grid_y, grid_z], radial_in, radial_out, mix_weight)
    updated = lax.map(update_one, jnp.arange(NXB * NYB * NZB).astype(jnp.int32))
    return updated.reshape(NXB, NYB, NZB, SLOTS, C)
```

```python
import functools
import math

import jax
import jax.numpy as jnp
from jax import lax
from jax.experimental import pallas as pl
from jax.experimental.pallas import tpu as pltpu
from jax.sharding import PartitionSpec as P

ROOT_THREE = math.sqrt(3.0)
ROOT_FIVE = math.sqrt(5.0)
ROOT_FIFTEEN = math.sqrt(15.0)
CUTOFF_BINS = 3.0
FLOOR_BINS = 0.25
AXES = ("gx", "gy", "gz")
MESH = pl.DeviceIdType.MESH
AROUND = [(dx, dz) for dz in (-1, 0, 1) for dx in (-1, 0, 1) if (dx, dz) != (0, 0)]
BF16 = jnp.bfloat16
F32 = jnp.float32


def sin_pi(value):
    whole = jnp.floor(value + 0.5)
    r = value - whole
    odd = whole - 2.0 * jnp.floor(0.5 * whole)
    square = r * r
    total = jnp.full_like(r, -(math.pi**11) / math.factorial(11))
    for power in (9, 7, 5, 3, 1):
        sign = 1.0 if power % 4 == 1 else -1.0
        total = total * square + sign * math.pi**power / math.factorial(power)
    return (1.0 - 2.0 * odd) * r * total


def kernel(
    sizes,
    feats,
    offs,
    lists,
    pairs,
    counts,
    radial_in,
    radial_out,
    mix_weight,
    out,
    ext,
    places,
    hot_in,
    hot_out,
    halves,
    spread,
    radial,
    gathered,
    own_sem,
    send_sem,
    recv_sem,
):
    size_x, size_y, size_z = sizes
    me_x, me_y, me_z = (lax.axis_index(axis) for axis in AXES)
    z_first, z_last = size_z // 4, size_z // 4 + size_z // 2 - 1
    live = (me_z >= z_first) & (me_z <= z_last)
    below, above = me_z > z_first, me_z < z_last

    def has(dz):
        return {-1: below, 0: me_z >= 0, 1: above}[dz]

    def at(dx, dy, dz):
        return (
            lax.rem(me_x + dx + size_x, size_x),
            lax.rem(me_y + dy + size_y, size_y),
            lax.rem(me_z + dz + size_z, size_z),
        )

    def remote(number, source, target, device):
        return pltpu.make_async_remote_copy(
            src_ref=source,
            dst_ref=target,
            send_sem=send_sem.at[number],
            recv_sem=recv_sem.at[number],
            device_id=device,
            device_id_type=MESH,
        )

    z_from = {-1: pl.ds(0, 1), 0: pl.ds(0, 2), 1: pl.ds(1, 1)}
    z_from_ext = {-1: pl.ds(1, 1), 0: pl.ds(1, 2), 1: pl.ds(2, 1)}
    z_to = {-1: pl.ds(3, 1), 0: pl.ds(1, 2), 1: pl.ds(0, 1)}

    place_y = [
        remote(0, places.at[1, 1, 2], places.at[1, 1, 0], at(0, 1, 0)),
        remote(1, places.at[1, 1, 1], places.at[1, 1, 3], at(0, -1, 0)),
    ]
    feat_y = [
        remote(2, feats.at[0, 1], ext.at[1, 0, pl.ds(1, 2)], at(0, 1, 0)),
        remote(3, feats.at[0, 0], ext.at[1, 3, pl.ds(1, 2)], at(0, -1, 0)),
    ]
    place_around = [
        remote(4 + n, places.at[1, 1], places.at[1 - dx, 1 - dz], at(dx, 0, dz))
        for n, (dx, dz) in enumerate(AROUND)
    ]
    feat_own = [
        remote(
            12 + n,
            feats.at[0, pl.ds(0, 2), z_from[dz]],
            ext.at[1 - dx, pl.ds(1, 2), z_to[dz]],
            at(dx, 0, dz),
        )
        for n, (dx, dz) in enumerate(AROUND)
    ]

    def feat_relay(slot):
        row = 3 * slot
        return [
            remote(
                20 + 8 * slot + n,
                ext.at[1, row, z_from_ext[dz]],
                ext.at[1 - dx, row, z_to[dz]],
                at(dx, 0, dz),
            )
            for n, (dx, dz) in enumerate(AROUND)
        ]

    def start_around(copies):
        for (dx, dz), copy in zip(AROUND, copies):
            pl.when(has(dz))(copy.start)

    def recv_around(copies):
        for (dx, dz), copy in zip(AROUND, copies):
            pl.when(has(-dz))(copy.wait_recv)

    def send_around(copies):
        for (dx, dz), copy in zip(AROUND, copies):
            pl.when(has(dz))(copy.wait_send)

    def lists_of(b):
        hy, hz = b // 2, b % 2
        flat = lists[0, hy, hz]
        digit = flat >> 7
        step_x = (digit * 57) >> 9
        rest = digit - 9 * step_x
        step_y = (rest * 11) >> 5
        step_z = rest - 3 * step_y
        return flat & 127, digit, step_x, step_y, step_z

    lane = lax.broadcasted_iota(jnp.int32, (8, 128), 1)
    row = lax.broadcasted_iota(jnp.int32, (8, 128), 0)

    def one_hots(b):
        hy, hz = b // 2, b % 2
        slot, _, step_x, step_y, step_z = lists_of(b)
        used = row < pairs[0, hy, pl.ds(hz, 1), :]
        layer = step_y - 1 + hy
        inner = (layer == 0) | (layer == 1)
        around = step_x * 3 + step_z
        t_in = jnp.where(used & inner, around, -1)
        t_out = jnp.where(used & jnp.logical_not(inner), around, -1)
        slot_col = slot.astype(F32).T
        in_col = t_in.astype(F32).T
        out_col = t_out.astype(F32).T
        halves[b] = layer.astype(F32).T
        lanes = lax.broadcasted_iota(jnp.int32, (128, 128), 1).astype(F32).astype(BF16)
        zero = jnp.zeros((128, 128), BF16)
        for k in range(8):
            rows = pl.ds(128 * k, 128)

            def spread_col(col):
                return jnp.broadcast_to(col[:, k : k + 1], (128, 128)).astype(BF16)

            slots = jnp.where(spread_col(slot_col) == lanes, jnp.ones_like(zero), zero)
            in_k, out_k = spread_col(in_col), spread_col(out_col)
            for t in range(9):
                cols = pl.ds(128 * t, 128)
                hot_in[b, rows, cols] = jnp.where(in_k == float(t), slots, zero)
                hot_out[b, rows, cols] = jnp.where(out_k == float(t), slots, zero)

    def geometry(b):
        hy, hz = b // 2, b % 2
        slot, digit, step_x, step_y, step_z = lists_of(b)
        theirs = [jnp.zeros((8, 128), F32) for _ in range(3)]
        for d in range(27):
            dx, dy, dz = d // 9, d // 3 % 3, d % 3
            there = hz + dz
            chosen = digit == d
            for c in range(3):
                table = places[dx, (there + 1) // 2, hy + dy, pl.ds((there + 1) % 2 * 3 + c, 1), :]
                value = jnp.take_along_axis(jnp.broadcast_to(table, (8, 128)), slot, axis=1)
                theirs[c] = jnp.where(chosen, value, theirs[c])
        displace = []
        for c, step in enumerate((step_x, step_y, step_z)):
            own = places[1, 1, 1 + hy, pl.ds(hz * 3 + c, 1), :]
            displace.append((step - 1).astype(F32) + theirs[c] - own)
        x, y, z = displace
        distance = jnp.sqrt(x * x + y * y + z * z)
        floored = jnp.maximum(distance, FLOOR_BINS)
        u = jnp.minimum(distance / CUTOFF_BINS, 1.0)
        cube = u * u * u
        envelope = 1.0 - 10.0 * cube + 15.0 * cube * u - 6.0 * cube * u * u
        height = envelope / floored

        def along(value):
            return jnp.concatenate(
                [jnp.broadcast_to(value[k : k + 1, :], (8, 128)) for k in range(8)], axis=1
            )

        order = (lax.broadcasted_iota(jnp.int32, (8, 1024), 0) + 1).astype(F32)
        basis = sin_pi(order * along(u)) * along(height)
        before = jnp.dot(
            radial_in[...].T, basis, precision=lax.Precision.HIGHEST, preferred_element_type=F32
        )
        hidden = (0.5 * before * (1.0 + jnp.tanh(0.5 * before))).T.astype(BF16)
        radial[b] = jnp.dot(hidden, radial_out[...], preferred_element_type=F32).astype(BF16)

        pick = (row >> 1) * 32 + (lane & 31)
        k_here = (row & 1) * 4 + (lane >> 5)

        def regroup(value):
            total = jnp.zeros((8, 128), F32)
            for k in range(8):
                moved = jnp.take_along_axis(
                    jnp.broadcast_to(value[k : k + 1, :], (8, 128)), pick, axis=1
                )
                total = jnp.where(k_here == k, moved, total)
            return total

        x, y, z = (regroup(part / floored) for part in (x, y, z))
        harmonic = [
            ROOT_THREE * x,
            ROOT_THREE * y,
            ROOT_THREE * z,
            ROOT_FIFTEEN * x * y,
            ROOT_FIFTEEN * y * z,
            ROOT_FIFTEEN * z * x,
            0.5 * ROOT_FIVE * (3.0 * z * z - 1.0),
            0.5 * ROOT_FIFTEEN * (x * x - y * y),
        ]
        diagonal = (lax.broadcasted_iota(jnp.int32, (32, 128), 1) & 31) == (
            lax.broadcasted_iota(jnp.int32, (32, 128), 0)
        )
        for m in range(8):
            scaled = harmonic[m] * 8.0**-0.5
            for group in range(4):
                for part in range(2):
                    r = 2 * group + part
                    block = jnp.where(
                        diagonal, jnp.broadcast_to(scaled[r : r + 1, :], (32, 128)), 0.0
                    )
                    spread[b, group, pl.ds(32 * m, 32), pl.ds(128 * part, 128)] = block.astype(BF16)

    def gather_inner(b):
        hz = b % 2
        table = jnp.concatenate(
            [
                jnp.concatenate([ext[dx, 1, hz + dz], ext[dx, 2, hz + dz]], axis=1)
                for dx in range(3)
                for dz in range(3)
            ],
            axis=0,
        )
        both = jnp.dot(hot_in[b], table, preferred_element_type=F32)
        for k in range(8):
            part = both[128 * k : 128 * (k + 1)]
            upper = jnp.broadcast_to(halves[b, :, k : k + 1], (128, 128)) > 0.5
            gathered[b, pl.ds(128 * k, 128)] = jnp.where(upper, part[:, 128:], part[:, :128])

    def finish(b):
        hy, hz = b // 2, b % 2
        table = jnp.concatenate(
            [ext[dx, 3 * hy, hz + dz] for dx in range(3) for dz in range(3)], axis=0
        )
        theirs = gathered[b] + jnp.dot(hot_out[b], table, preferred_element_type=F32)
        first = radial[b, :, 0:128].astype(F32) * theirs
        total = first[0:128]
        for k in range(1, 8):
            total = total + first[128 * k : 128 * (k + 1)]
        scalar_part = (total * 8.0**-0.5).astype(BF16)
        vector = (radial[b, :, 128:256].astype(F32) * theirs).astype(BF16)
        tensor = (radial[b, :, 256:384].astype(F32) * theirs).astype(BF16)
        norms = [[], []]
        for group in range(4):
            for which, (product, first_m, last_m) in enumerate(((vector, 0, 3), (tensor, 3, 8))):
                part = jnp.concatenate(
                    [product[128 * k + 32 * group : 128 * k + 32 * group + 32] for k in range(8)],
                    axis=0,
                )
                amp = jnp.dot(
                    spread[b, group, pl.ds(32 * first_m, 32 * (last_m - first_m)), :],
                    part,
                    preferred_element_type=F32,
                )
                norm = None
                for m in range(last_m - first_m):
                    piece = amp[32 * m : 32 * (m + 1)]
                    norm = piece * piece if norm is None else norm + piece * piece
                norms[which].append(norm.astype(BF16))
        joined = jnp.concatenate(
            [
                ext[1, 1 + hy, 1 + hz],
                scalar_part,
                jnp.concatenate(norms[0], axis=0),
                jnp.concatenate(norms[1], axis=0),
            ],
            axis=1,
        )
        mixed = jnp.dot(joined, mix_weight[...], preferred_element_type=F32)
        live_slot = lax.broadcasted_iota(jnp.int32, (128, 128), 0) < counts[0, hy, hz]
        out[0, hy, hz] = jnp.where(live_slot, mixed, 0.0).astype(BF16)

    def each_bin(body):
        def step(b, carry):
            body(b)
            return carry

        lax.fori_loop(0, 4, step, 0)

    @pl.when(jnp.logical_not(live))
    def _():
        out[...] = jnp.zeros_like(out)

    @pl.when(live)
    def _():
        barrier = pltpu.get_barrier_semaphore()
        for dy in (-1, 1):
            pl.semaphore_signal(barrier, inc=1, device_id=at(0, dy, 0), device_id_type=MESH)
        for dx, dz in AROUND:

            @pl.when(has(dz))
            def _():
                pl.semaphore_signal(barrier, inc=1, device_id=at(dx, 0, dz), device_id_type=MESH)

        own_copy = pltpu.make_async_copy(feats.at[0], ext.at[1, pl.ds(1, 2), pl.ds(1, 2)], own_sem)
        own_copy.start()
        for y in range(2):
            for c in range(3):
                value = offs[0, y, c].astype(F32)
                for z in range(2):
                    places[1, 1, 1 + y, 3 * z + c : 3 * z + c + 1, :] = value[z : z + 1]
            places[1, 1, 1 + y, 6:8, :] = jnp.zeros((2, 128), F32)
        pl.semaphore_wait(
            barrier, 4 + 3 * below.astype(jnp.int32) + 3 * above.astype(jnp.int32)
        )
        for copy in place_y + feat_y:
            copy.start()
        start_around(feat_own)

        @pl.when(jnp.logical_not(below))
        def _():
            ext[:, :, 0] = jnp.zeros((3, 4, 128, 128), BF16)

        @pl.when(jnp.logical_not(above))
        def _():
            ext[:, :, 3] = jnp.zeros((3, 4, 128, 128), BF16)

        each_bin(one_hots)
        for copy in place_y:
            copy.wait_recv()
        start_around(place_around)
        early = lax.rem(me_y, 2)

        def relay(slot):
            feat_y[slot].wait_recv()
            start_around(feat_relay(slot))

        pl.when(early == 0)(functools.partial(relay, 1))
        pl.when(early == 1)(functools.partial(relay, 0))
        recv_around(place_around)
        each_bin(geometry)
        pl.when(early == 0)(functools.partial(relay, 0))
        pl.when(early == 1)(functools.partial(relay, 1))
        own_copy.wait()
        recv_around(feat_own)
        each_bin(gather_inner)
        recv_around(feat_relay(0))
        recv_around(feat_relay(1))
        each_bin(finish)
        for copy in place_y + feat_y:
            copy.wait_send()
        for copies in (place_around, feat_own, feat_relay(0), feat_relay(1)):
            send_around(copies)


def per_device(sizes, *arrays):
    node_feats, offsets, counts, neighbours, pair_counts, radial_in, radial_out, mix_weight = arrays
    vmem = pl.BlockSpec(memory_space=pltpu.VMEM)
    return pl.pallas_call(
        functools.partial(kernel, sizes),
        out_shape=jax.ShapeDtypeStruct(node_feats.shape, BF16),
        in_specs=[
            pl.BlockSpec(memory_space=pl.ANY),
            vmem,
            vmem,
            vmem,
            pl.BlockSpec(memory_space=pltpu.SMEM),
            vmem,
            vmem,
            vmem,
        ],
        out_specs=vmem,
        scratch_shapes=[
            pltpu.VMEM((3, 4, 4, 128, 128), BF16),
            pltpu.VMEM((3, 3, 4, 8, 128), F32),
            pltpu.VMEM((4, 1024, 1152), BF16),
            pltpu.VMEM((4, 1024, 1152), BF16),
            pltpu.VMEM((4, 128, 8), F32),
            pltpu.VMEM((4, 4, 256, 256), BF16),
            pltpu.VMEM((4, 1024, 384), BF16),
            pltpu.VMEM((4, 1024, 128), F32),
            pltpu.SemaphoreType.DMA,
            pltpu.SemaphoreType.DMA((36,)),
            pltpu.SemaphoreType.DMA((36,)),
        ],
        compiler_params=pltpu.CompilerParams(
            collective_id=0, has_side_effects=True, vmem_limit_bytes=50 * 1024 * 1024
        ),
        cost_estimate=pl.CostEstimate(
            flops=4_000_000_000, bytes_accessed=4_000_000, transcendentals=600_000
        ),
    )(
        node_feats,
        jnp.transpose(offsets, (0, 1, 3, 2, 4)),
        jnp.swapaxes(neighbours, 3, 4),
        pair_counts,
        counts,
        radial_in,
        radial_out,
        mix_weight,
    )


def solution(mesh):
    placed = (
        P("gx", "gy", "gz", None, None),
        P("gx", "gy", "gz", None, None),
        P("gx", "gy", "gz"),
        P("gx", "gy", "gz", None, None),
        P("gx", "gy", "gz", None),
        P(),
        P(),
        P(),
    )
    sizes = tuple(mesh.shape[axis] for axis in AXES)
    return jax.shard_map(
        functools.partial(per_device, sizes),
        mesh=mesh,
        in_specs=placed,
        out_specs=P("gx", "gy", "gz", None, None),
        check_vma=False,
    )
```

```python
import functools
import math

import jax
import jax.numpy as jnp
from jax import lax
from jax.experimental import pallas as pl
from jax.experimental.pallas import tpu as pltpu
from jax.sharding import PartitionSpec as P

ROOT_THREE = math.sqrt(3.0)
ROOT_FIVE = math.sqrt(5.0)
ROOT_FIFTEEN = math.sqrt(15.0)
CUTOFF_BINS = 3.0
FLOOR_BINS = 0.25
AXES = ("gx", "gy", "gz")
MESH = pl.DeviceIdType.MESH
AROUND = [(dx, dz) for dz in (-1, 0, 1) for dx in (-1, 0, 1) if (dx, dz) != (0, 0)]
BF16 = jnp.bfloat16
F32 = jnp.float32


def sin_pi(value):
    whole = jnp.floor(value + 0.5)
    r = value - whole
    odd = whole - 2.0 * jnp.floor(0.5 * whole)
    square = r * r
    total = jnp.full_like(r, -(math.pi**11) / math.factorial(11))
    for power in (9, 7, 5, 3, 1):
        sign = 1.0 if power % 4 == 1 else -1.0
        total = total * square + sign * math.pi**power / math.factorial(power)
    return (1.0 - 2.0 * odd) * r * total


def kernel(
    sizes,
    feats,
    offs_in,
    lists_in,
    pairs_in,
    counts,
    radial_in_in,
    radial_out_in,
    mix_weight_in,
    out,
    offs,
    lists,
    pairs,
    radial_in,
    radial_out,
    mix_weight,
    ext,
    places,
    hot_in,
    hot_out,
    halves,
    spread,
    radial,
    gathered,
    own_sem,
    input_sem,
    send_sem,
    recv_sem,
    far_sem,
):
    size_x, size_y, size_z = sizes
    me_x, me_y, me_z = (lax.axis_index(axis) for axis in AXES)
    z_first, z_last = size_z // 4, size_z // 4 + size_z // 2 - 1
    live = (me_z >= z_first) & (me_z <= z_last)
    below, above = me_z > z_first, me_z < z_last

    def has(dz):
        return {-1: below, 0: me_z >= 0, 1: above}[dz]

    def at(dx, dy, dz):
        return (
            lax.rem(me_x + dx + size_x, size_x),
            lax.rem(me_y + dy + size_y, size_y),
            lax.rem(me_z + dz + size_z, size_z),
        )

    def remote(number, source, target, device):
        return pltpu.make_async_remote_copy(
            src_ref=source,
            dst_ref=target,
            send_sem=send_sem.at[number],
            recv_sem=recv_sem.at[number],
            device_id=device,
            device_id_type=MESH,
        )

    z_from = {-1: pl.ds(0, 1), 0: pl.ds(0, 2), 1: pl.ds(1, 1)}
    z_from_ext = {-1: pl.ds(1, 1), 0: pl.ds(1, 2), 1: pl.ds(2, 1)}
    z_to = {-1: pl.ds(3, 1), 0: pl.ds(1, 2), 1: pl.ds(0, 1)}

    late = lax.rem(me_y, 2)
    early = 1 - late
    far_step = 2 * late - 1

    def to_y(first, source, target, slot):
        return remote(first + slot, source, target, at(0, 2 * slot - 1, 0))

    def place_y(slot):
        return to_y(0, places.at[1, 1, 1 + slot], places.at[1, 1, 3 - 3 * slot], slot)

    def feat_y(slot):
        return to_y(2, feats.at[0, slot], ext.at[1, 3 - 3 * slot, pl.ds(1, 2)], slot)

    def around(first, source, target):
        return [
            remote(first + n, source(dx, dz), target(dx, dz), at(dx, 0, dz))
            for n, (dx, dz) in enumerate(AROUND)
        ]

    def place_early():
        rows = pl.ds(early, 3)
        return around(
            4,
            lambda dx, dz: places.at[1, 1, rows],
            lambda dx, dz: places.at[1 - dx, 1 - dz, rows],
        )

    def place_late():
        return around(
            12,
            lambda dx, dz: places.at[1, 1, 3 * late],
            lambda dx, dz: places.at[1 - dx, 1 - dz, 3 * late],
        )

    def feat_own():
        return around(
            20,
            lambda dx, dz: feats.at[0, pl.ds(0, 2), z_from[dz]],
            lambda dx, dz: ext.at[1 - dx, pl.ds(1, 2), z_to[dz]],
        )

    def feat_relay(first, slot):
        return around(
            first,
            lambda dx, dz: ext.at[1, 3 * slot, z_from_ext[dz]],
            lambda dx, dz: ext.at[1 - dx, 3 * slot, z_to[dz]],
        )

    def feat_early():
        return feat_relay(28, early)

    def feat_late():
        return feat_relay(36, late)

    def start_around(copies):
        for (dx, dz), copy in zip(AROUND, copies):
            pl.when(has(dz))(copy.start)

    def recv_around(copies):
        for (dx, dz), copy in zip(AROUND, copies):
            pl.when(has(-dz))(copy.wait_recv)

    def send_around(copies):
        for (dx, dz), copy in zip(AROUND, copies):
            pl.when(has(dz))(copy.wait_send)

    def lists_of(b):
        hy, hz = b // 2, b % 2
        flat = lists[0, hy, hz]
        digit = flat >> 7
        step_x = (digit * 57) >> 9
        rest = digit - 9 * step_x
        step_y = (rest * 11) >> 5
        step_z = rest - 3 * step_y
        return flat & 127, digit, step_x, step_y, step_z

    lane = lax.broadcasted_iota(jnp.int32, (8, 128), 1)
    row = lax.broadcasted_iota(jnp.int32, (8, 128), 0)

    def one_hots(b):
        hy, hz = b // 2, b % 2
        slot, _, step_x, step_y, step_z = lists_of(b)
        used = row < pairs[0, hy, pl.ds(hz, 1), :]
        layer = step_y - 1 + hy
        inner = (layer == 0) | (layer == 1)
        around = step_x * 3 + step_z
        t_in = jnp.where(used & inner, around, -1)
        t_out = jnp.where(used & jnp.logical_not(inner), around, -1)
        slot_col = slot.astype(F32).T
        in_col = t_in.astype(F32).T
        out_col = t_out.astype(F32).T
        halves[b] = layer.astype(F32).T
        lanes = lax.broadcasted_iota(jnp.int32, (128, 128), 1).astype(F32).astype(BF16)
        zero = jnp.zeros((128, 128), BF16)
        for k in range(8):
            rows = pl.ds(128 * k, 128)

            def spread_col(col):
                return jnp.broadcast_to(col[:, k : k + 1], (128, 128)).astype(BF16)

            slots = jnp.where(spread_col(slot_col) == lanes, jnp.ones_like(zero), zero)
            in_k, out_k = spread_col(in_col), spread_col(out_col)
            for t in range(9):
                cols = pl.ds(128 * t, 128)
                hot_in[b, rows, cols] = jnp.where(in_k == float(t), slots, zero)
                hot_out[b, rows, cols] = jnp.where(out_k == float(t), slots, zero)

    def geometry(b):
        hy, hz = b // 2, b % 2
        slot, digit, step_x, step_y, step_z = lists_of(b)
        theirs = [jnp.zeros((8, 128), F32) for _ in range(3)]
        for d in range(27):
            dx, dy, dz = d // 9, d // 3 % 3, d % 3
            there = hz + dz
            chosen = digit == d
            for c in range(3):
                table = places[dx, (there + 1) // 2, hy + dy, pl.ds((there + 1) % 2 * 3 + c, 1), :]
                value = jnp.take_along_axis(jnp.broadcast_to(table, (8, 128)), slot, axis=1)
                theirs[c] = jnp.where(chosen, value, theirs[c])
        displace = []
        for c, step in enumerate((step_x, step_y, step_z)):
            own = places[1, 1, 1 + hy, pl.ds(hz * 3 + c, 1), :]
            displace.append((step - 1).astype(F32) + theirs[c] - own)
        x, y, z = displace
        distance = jnp.sqrt(x * x + y * y + z * z)
        floored = jnp.maximum(distance, FLOOR_BINS)
        u = jnp.minimum(distance / CUTOFF_BINS, 1.0)
        cube = u * u * u
        envelope = 1.0 - 10.0 * cube + 15.0 * cube * u - 6.0 * cube * u * u
        height = envelope / floored

        def along(value):
            return jnp.concatenate(
                [jnp.broadcast_to(value[k : k + 1, :], (8, 128)) for k in range(8)], axis=1
            )

        order = (lax.broadcasted_iota(jnp.int32, (8, 1024), 0) + 1).astype(F32)
        basis = sin_pi(order * along(u)) * along(height)
        before = jnp.dot(
            radial_in[...].T, basis, precision=lax.Precision.HIGHEST, preferred_element_type=F32
        )
        hidden = (0.5 * before * (1.0 + jnp.tanh(0.5 * before))).T.astype(BF16)
        radial[b] = jnp.dot(hidden, radial_out[...], preferred_element_type=F32).astype(BF16)

        pick = (row >> 1) * 32 + (lane & 31)
        k_here = (row & 1) * 4 + (lane >> 5)

        def regroup(value):
            total = jnp.zeros((8, 128), F32)
            for k in range(8):
                moved = jnp.take_along_axis(
                    jnp.broadcast_to(value[k : k + 1, :], (8, 128)), pick, axis=1
                )
                total = jnp.where(k_here == k, moved, total)
            return total

        x, y, z = (regroup(part / floored) for part in (x, y, z))
        harmonic = [
            ROOT_THREE * x,
            ROOT_THREE * y,
            ROOT_THREE * z,
            ROOT_FIFTEEN * x * y,
            ROOT_FIFTEEN * y * z,
            ROOT_FIFTEEN * z * x,
            0.5 * ROOT_FIVE * (3.0 * z * z - 1.0),
            0.5 * ROOT_FIFTEEN * (x * x - y * y),
        ]
        diagonal = (lax.broadcasted_iota(jnp.int32, (32, 128), 1) & 31) == (
            lax.broadcasted_iota(jnp.int32, (32, 128), 0)
        )
        for m in range(8):
            scaled = harmonic[m] * 8.0**-0.5
            for group in range(4):
                for part in range(2):
                    r = 2 * group + part
                    block = jnp.where(
                        diagonal, jnp.broadcast_to(scaled[r : r + 1, :], (32, 128)), 0.0
                    )
                    spread[b, group, pl.ds(32 * m, 32), pl.ds(128 * part, 128)] = block.astype(BF16)

    def gather_inner(b):
        hz = b % 2
        table = jnp.concatenate(
            [
                jnp.concatenate([ext[dx, 1, hz + dz], ext[dx, 2, hz + dz]], axis=1)
                for dx in range(3)
                for dz in range(3)
            ],
            axis=0,
        )
        both = jnp.dot(hot_in[b], table, preferred_element_type=F32)
        for k in range(8):
            part = both[128 * k : 128 * (k + 1)]
            upper = jnp.broadcast_to(halves[b, :, k : k + 1], (128, 128)) > 0.5
            gathered[b, pl.ds(128 * k, 128)] = jnp.where(upper, part[:, 128:], part[:, :128])

    def finish(b):
        hy, hz = b // 2, b % 2
        table = jnp.concatenate(
            [ext[dx, 3 * hy, hz + dz] for dx in range(3) for dz in range(3)], axis=0
        )
        theirs = gathered[b] + jnp.dot(hot_out[b], table, preferred_element_type=F32)
        first = radial[b, :, 0:128].astype(F32) * theirs
        total = first[0:128]
        for k in range(1, 8):
            total = total + first[128 * k : 128 * (k + 1)]
        scalar_part = (total * 8.0**-0.5).astype(BF16)
        vector = (radial[b, :, 128:256].astype(F32) * theirs).astype(BF16)
        tensor = (radial[b, :, 256:384].astype(F32) * theirs).astype(BF16)
        norms = [[], []]
        for group in range(4):
            for which, (product, first_m, last_m) in enumerate(((vector, 0, 3), (tensor, 3, 8))):
                part = jnp.concatenate(
                    [product[128 * k + 32 * group : 128 * k + 32 * group + 32] for k in range(8)],
                    axis=0,
                )
                amp = jnp.dot(
                    spread[b, group, pl.ds(32 * first_m, 32 * (last_m - first_m)), :],
                    part,
                    preferred_element_type=F32,
                )
                norm = None
                for m in range(last_m - first_m):
                    piece = amp[32 * m : 32 * (m + 1)]
                    norm = piece * piece if norm is None else norm + piece * piece
                norms[which].append(norm.astype(BF16))
        joined = jnp.concatenate(
            [
                ext[1, 1 + hy, 1 + hz],
                scalar_part,
                jnp.concatenate(norms[0], axis=0),
                jnp.concatenate(norms[1], axis=0),
            ],
            axis=1,
        )
        mixed = jnp.dot(joined, mix_weight[...], preferred_element_type=F32)
        live_slot = lax.broadcasted_iota(jnp.int32, (128, 128), 0) < counts[0, hy, hz]
        out[0, hy, hz] = jnp.where(live_slot, mixed, 0.0).astype(BF16)

    def each_bin(body, hy=None):
        def step(b, carry):
            body(b if hy is None else 2 * hy + b)
            return carry

        lax.fori_loop(0, 4 if hy is None else 2, step, 0)

    def greet(barrier, device):
        pl.semaphore_signal(barrier, inc=1, device_id=device, device_id_type=MESH)

    half_y = size_y // 2
    upper = me_y // half_y
    in_half = lax.rem(me_y, half_y)
    at_edge = (in_half == 0) | (in_half == half_y - 1)
    first_far, second_far = at_edge & (upper == 0), at_edge & (upper == 1)
    idle_above = size_z - 1 - z_last

    def between(pair):
        low = pair < idle_above
        y_first = jnp.where(upper == 0, me_y, lax.rem(me_y + far_step + size_y, size_y))
        return (
            me_x,
            jnp.where(low, y_first, y_first + half_y),
            jnp.where(low, z_last + 1 + pair, pair - idle_above),
        )

    @pl.when(jnp.logical_not(live))
    def _():
        out[...] = jnp.zeros_like(out)
        low = (upper == 0) & (me_z > z_last)
        high = (upper == 1) & (me_z < z_first)

        @pl.when(at_edge & (low | high))
        def _():
            barrier = pltpu.get_barrier_semaphore()
            pair = jnp.where(low, me_z - z_last - 1, me_z + idle_above)
            pl.semaphore_wait(barrier, 2)
            pl.semaphore_signal(
                far_sem,
                inc=1,
                device_id=(me_x, me_y - half_y * upper, z_first + pair),
                device_id_type=MESH,
            )

    @pl.when(live)
    def _():
        barrier = pltpu.get_barrier_semaphore()
        pl.when(at_edge)(lambda: greet(barrier, between(me_z - z_first)))
        pl.when(jnp.logical_not(second_far))(lambda: greet(barrier, at(0, far_step, 0)))
        greet(barrier, at(0, -far_step, 0))
        for dx, dz in AROUND:
            pl.when(has(dz))(functools.partial(greet, barrier, at(dx, 0, dz)))

        inputs = [
            pltpu.make_async_copy(source, target, input_sem.at[n])
            for n, (source, target) in enumerate(
                (
                    (offs_in, offs),
                    (lists_in, lists),
                    (pairs_in, pairs),
                    (radial_in_in, radial_in),
                    (radial_out_in, radial_out),
                    (mix_weight_in, mix_weight),
                )
            )
        ]
        own_copy = pltpu.make_async_copy(feats.at[0], ext.at[1, pl.ds(1, 2), pl.ds(1, 2)], own_sem)
        for copy in inputs:
            copy.start()
        own_copy.start()
        inputs[0].wait()
        for y in range(2):
            for c in range(3):
                value = offs[0, y, c].astype(F32)
                for z in range(2):
                    places[1, 1, 1 + y, 3 * z + c : 3 * z + c + 1, :] = value[z : z + 1]
            places[1, 1, 1 + y, 6:8, :] = jnp.zeros((2, 128), F32)
        near = 3 + 3 * below.astype(jnp.int32) + 3 * above.astype(jnp.int32)
        pl.semaphore_wait(barrier, near + jnp.where(first_far, 0, 1))

        def send_far():
            place_y(late).start()
            feat_y(late).start()

        pl.when(jnp.logical_not(first_far))(send_far)
        place_y(early).start()
        feat_y(early).start()
        start_around(feat_own())

        @pl.when(jnp.logical_not(below))
        def _():
            ext[:, :, 0] = jnp.zeros((3, 4, 128, 128), BF16)

        @pl.when(jnp.logical_not(above))
        def _():
            ext[:, :, 3] = jnp.zeros((3, 4, 128, 128), BF16)

        for copy in inputs[1:]:
            copy.wait()
        each_bin(one_hots)
        place_y(1 - early).wait_recv()
        start_around(place_early())
        feat_y(1 - early).wait_recv()
        start_around(feat_early())
        own_copy.wait()
        recv_around(feat_own())
        each_bin(gather_inner)
        recv_around(place_early())
        each_bin(geometry, early)
        recv_around(feat_early())
        each_bin(finish, early)

        @pl.when(first_far)
        def _():
            pl.semaphore_wait(far_sem, 1)
            send_far()

        place_y(1 - late).wait_recv()
        start_around(place_late())
        feat_y(1 - late).wait_recv()
        start_around(feat_late())
        recv_around(place_late())
        each_bin(geometry, late)
        recv_around(feat_late())
        each_bin(finish, late)
        for slot in range(2):
            place_y(slot).wait_send()
            feat_y(slot).wait_send()
        for copies in (place_early, place_late, feat_own, feat_early, feat_late):
            send_around(copies())


def per_device(sizes, *arrays):
    node_feats, offsets, counts, neighbours, pair_counts, radial_in, radial_out, mix_weight = arrays
    hbm = pl.BlockSpec(memory_space=pl.ANY)
    return pl.pallas_call(
        functools.partial(kernel, sizes),
        out_shape=jax.ShapeDtypeStruct(node_feats.shape, BF16),
        in_specs=[hbm, hbm, hbm, hbm, pl.BlockSpec(memory_space=pltpu.SMEM), hbm, hbm, hbm],
        out_specs=pl.BlockSpec(memory_space=pltpu.VMEM),
        scratch_shapes=[
            pltpu.VMEM((1, 2, 3, 2, 128), BF16),
            pltpu.VMEM((1, 2, 2, 8, 128), jnp.int32),
            pltpu.VMEM((1, 2, 2, 128), jnp.int32),
            pltpu.VMEM((8, 64), F32),
            pltpu.VMEM((64, 384), BF16),
            pltpu.VMEM((512, 128), BF16),
            pltpu.VMEM((3, 4, 4, 128, 128), BF16),
            pltpu.VMEM((3, 3, 4, 8, 128), F32),
            pltpu.VMEM((4, 1024, 1152), BF16),
            pltpu.VMEM((4, 1024, 1152), BF16),
            pltpu.VMEM((4, 128, 8), F32),
            pltpu.VMEM((4, 4, 256, 256), BF16),
            pltpu.VMEM((4, 1024, 384), BF16),
            pltpu.VMEM((4, 1024, 128), F32),
            pltpu.SemaphoreType.DMA,
            pltpu.SemaphoreType.DMA((6,)),
            pltpu.SemaphoreType.DMA((44,)),
            pltpu.SemaphoreType.DMA((44,)),
            pltpu.SemaphoreType.REGULAR,
        ],
        compiler_params=pltpu.CompilerParams(
            collective_id=0, has_side_effects=True, vmem_limit_bytes=63 * 1024 * 1024
        ),
        cost_estimate=pl.CostEstimate(
            flops=4_000_000_000, bytes_accessed=4_000_000, transcendentals=600_000
        ),
    )(
        node_feats,
        jnp.transpose(offsets, (0, 1, 3, 2, 4)),
        jnp.swapaxes(neighbours, 3, 4),
        pair_counts,
        counts,
        radial_in,
        radial_out,
        mix_weight,
    )


def solution(mesh):
    placed = (
        P("gx", "gy", "gz", None, None),
        P("gx", "gy", "gz", None, None),
        P("gx", "gy", "gz"),
        P("gx", "gy", "gz", None, None),
        P("gx", "gy", "gz", None),
        P(),
        P(),
        P(),
    )
    sizes = tuple(mesh.shape[axis] for axis in AXES)
    return jax.shard_map(
        functools.partial(per_device, sizes),
        mesh=mesh,
        in_specs=placed,
        out_specs=P("gx", "gy", "gz", None, None),
        check_vma=False,
    )
```

```python
import functools
import math

import jax
import jax.numpy as jnp
from jax import lax
from jax.experimental import pallas as pl
from jax.experimental.pallas import tpu as pltpu
from jax.sharding import PartitionSpec as P

ROOT_THREE = math.sqrt(3.0)
ROOT_FIVE = math.sqrt(5.0)
ROOT_FIFTEEN = math.sqrt(15.0)
CUTOFF_BINS = 3.0
FLOOR_BINS = 0.25
AXES = ("gx", "gy", "gz")
MESH = pl.DeviceIdType.MESH
AROUND = [(dx, dz) for dz in (-1, 0, 1) for dx in (-1, 0, 1) if (dx, dz) != (0, 0)]
BF16 = jnp.bfloat16
F32 = jnp.float32


def sin_pi(value):
    whole = jnp.floor(value + 0.5)
    r = value - whole
    odd = whole - 2.0 * jnp.floor(0.5 * whole)
    square = r * r
    total = jnp.full_like(r, -(math.pi**11) / math.factorial(11))
    for power in (9, 7, 5, 3, 1):
        sign = 1.0 if power % 4 == 1 else -1.0
        total = total * square + sign * math.pi**power / math.factorial(power)
    return (1.0 - 2.0 * odd) * r * total


def kernel(
    sizes,
    feats,
    offs_in,
    lists_in,
    pairs_in,
    counts,
    radial_in_in,
    radial_out_in,
    mix_weight_in,
    out,
    result,
    offs,
    lists,
    pairs,
    radial_in,
    radial_out,
    mix_weight,
    ext,
    places,
    hot_in,
    hot_out,
    halves,
    spread,
    radial,
    gathered,
    own_sem,
    input_sem,
    send_sem,
    recv_sem,
    far_sem,
):
    size_x, size_y, size_z = sizes
    me_x, me_y, me_z = (lax.axis_index(axis) for axis in AXES)
    z_first, z_last = size_z // 4, size_z // 4 + size_z // 2 - 1
    live = (me_z >= z_first) & (me_z <= z_last)
    below, above = me_z > z_first, me_z < z_last

    def has(dz):
        return {-1: below, 0: me_z >= 0, 1: above}[dz]

    def at(dx, dy, dz):
        return (
            lax.rem(me_x + dx + size_x, size_x),
            lax.rem(me_y + dy + size_y, size_y),
            lax.rem(me_z + dz + size_z, size_z),
        )

    def remote(number, source, target, device):
        return pltpu.make_async_remote_copy(
            src_ref=source,
            dst_ref=target,
            send_sem=send_sem.at[number],
            recv_sem=recv_sem.at[number],
            device_id=device,
            device_id_type=MESH,
        )

    z_from = {-1: pl.ds(1, 1), 0: pl.ds(1, 2), 1: pl.ds(2, 1)}
    z_to = {-1: pl.ds(3, 1), 0: pl.ds(1, 2), 1: pl.ds(0, 1)}

    late = lax.rem(me_y, 2)
    early = 1 - late
    far_step = 2 * late - 1

    def to_y(first, source, target, slot):
        return remote(first + slot, source, target, at(0, 2 * slot - 1, 0))

    def place_y(slot):
        return to_y(0, places.at[1, 1, 1 + slot], places.at[1, 1, 3 - 3 * slot], slot)

    def feat_y(slot):
        return to_y(
            2, ext.at[1, 1 + slot, pl.ds(1, 2)], ext.at[1, 3 - 3 * slot, pl.ds(1, 2)], slot
        )

    def feat_far(slot):
        return [
            remote(
                46 + z,
                ext.at[1, 1 + slot, 1 + z],
                ext.at[1, 3 - 3 * slot, 1 + z],
                at(0, 2 * slot - 1, 0),
            )
            for z in range(2)
        ]

    def around(first, source, target):
        return [
            remote(first + n, source(dx, dz), target(dx, dz), at(dx, 0, dz))
            for n, (dx, dz) in enumerate(AROUND)
        ]

    def place_early():
        rows = pl.ds(early, 3)
        return around(
            4,
            lambda dx, dz: places.at[1, 1, rows],
            lambda dx, dz: places.at[1 - dx, 1 - dz, rows],
        )

    def place_late():
        return around(
            12,
            lambda dx, dz: places.at[1, 1, 3 * late],
            lambda dx, dz: places.at[1 - dx, 1 - dz, 3 * late],
        )

    def feat_own():
        return around(
            20,
            lambda dx, dz: ext.at[1, pl.ds(1, 2), z_from[dz]],
            lambda dx, dz: ext.at[1 - dx, pl.ds(1, 2), z_to[dz]],
        )

    def feat_early():
        row = 3 * early
        return around(
            28,
            lambda dx, dz: ext.at[1, row, z_from[dz]],
            lambda dx, dz: ext.at[1 - dx, row, z_to[dz]],
        )

    def feat_late(z):
        row = 3 * late
        side = 2 * z - 1
        return [
            (
                dz,
                remote(
                    36 + 5 * z + n,
                    ext.at[1, row, 1 + z],
                    ext.at[1 - dx, row, 1 + z if dz == 0 else 3 - 3 * z],
                    at(dx, 0, dz),
                ),
            )
            for n, (dx, dz) in enumerate(((0, side), (-1, side), (1, side), (-1, 0), (1, 0)))
        ]

    def start_around(copies):
        for (dx, dz), copy in zip(AROUND, copies):
            pl.when(has(dz))(copy.start)

    def recv_around(copies):
        for (dx, dz), copy in zip(AROUND, copies):
            pl.when(has(-dz))(copy.wait_recv)

    def send_around(copies):
        for (dx, dz), copy in zip(AROUND, copies):
            pl.when(has(dz))(copy.wait_send)

    def lists_of(b):
        hy, hz = b // 2, b % 2
        flat = lists[0, hy, hz]
        digit = flat >> 7
        step_x = (digit * 57) >> 9
        rest = digit - 9 * step_x
        step_y = (rest * 11) >> 5
        step_z = rest - 3 * step_y
        return flat & 127, digit, step_x, step_y, step_z

    lane = lax.broadcasted_iota(jnp.int32, (8, 128), 1)
    row = lax.broadcasted_iota(jnp.int32, (8, 128), 0)

    def one_hots(b):
        hy, hz = b // 2, b % 2
        slot, _, step_x, step_y, step_z = lists_of(b)
        used = row < pairs[0, hy, pl.ds(hz, 1), :]
        layer = step_y - 1 + hy
        inner = (layer == 0) | (layer == 1)
        around = step_x * 3 + step_z
        t_in = jnp.where(used & inner, around, -1)
        column = step_x == 1
        beyond = column & (step_z == 2 * hz)
        chunk = jnp.where(column, jnp.where(beyond, 3, 4), step_z)
        t_out = jnp.where(used & jnp.logical_not(inner), chunk, -1)
        side = jnp.where(column, jnp.where(beyond, 0, step_z - 1 + hz), step_x >> 1)
        slot_col = slot.astype(F32).T
        in_col = t_in.astype(F32).T
        out_col = t_out.astype(F32).T
        halves[b] = jnp.where(inner, layer, side).astype(F32).T
        lanes = lax.broadcasted_iota(jnp.int32, (128, 128), 1).astype(F32).astype(BF16)
        zero = jnp.zeros((128, 128), BF16)
        for k in range(8):
            rows = pl.ds(128 * k, 128)

            def spread_col(col):
                return jnp.broadcast_to(col[:, k : k + 1], (128, 128)).astype(BF16)

            slots = jnp.where(spread_col(slot_col) == lanes, jnp.ones_like(zero), zero)
            in_k, out_k = spread_col(in_col), spread_col(out_col)
            for t in range(9):
                cols = pl.ds(128 * t, 128)
                hot_in[b, rows, cols] = jnp.where(in_k == float(t), slots, zero)
                if t < 5:
                    hot_out[b, rows, cols] = jnp.where(out_k == float(t), slots, zero)

    def geometry(b):
        hy, hz = b // 2, b % 2
        slot, digit, step_x, step_y, step_z = lists_of(b)
        theirs = [jnp.zeros((8, 128), F32) for _ in range(3)]
        for d in range(27):
            dx, dy, dz = d // 9, d // 3 % 3, d % 3
            there = hz + dz
            chosen = digit == d
            for c in range(3):
                table = places[dx, (there + 1) // 2, hy + dy, pl.ds((there + 1) % 2 * 3 + c, 1), :]
                value = jnp.take_along_axis(jnp.broadcast_to(table, (8, 128)), slot, axis=1)
                theirs[c] = jnp.where(chosen, value, theirs[c])
        displace = []
        for c, step in enumerate((step_x, step_y, step_z)):
            own = places[1, 1, 1 + hy, pl.ds(hz * 3 + c, 1), :]
            displace.append((step - 1).astype(F32) + theirs[c] - own)
        x, y, z = displace
        distance = jnp.sqrt(x * x + y * y + z * z)
        floored = jnp.maximum(distance, FLOOR_BINS)
        u = jnp.minimum(distance / CUTOFF_BINS, 1.0)
        cube = u * u * u
        envelope = 1.0 - 10.0 * cube + 15.0 * cube * u - 6.0 * cube * u * u
        height = envelope / floored

        def along(value):
            return jnp.concatenate(
                [jnp.broadcast_to(value[k : k + 1, :], (8, 128)) for k in range(8)], axis=1
            )

        order = (lax.broadcasted_iota(jnp.int32, (8, 1024), 0) + 1).astype(F32)
        basis = sin_pi(order * along(u)) * along(height)
        before = jnp.dot(
            radial_in[...].T, basis, precision=lax.Precision.HIGHEST, preferred_element_type=F32
        )
        hidden = (0.5 * before * (1.0 + jnp.tanh(0.5 * before))).T.astype(BF16)
        radial[b] = jnp.dot(hidden, radial_out[...], preferred_element_type=F32).astype(BF16)

        pick = (row >> 1) * 32 + (lane & 31)
        k_here = (row & 1) * 4 + (lane >> 5)

        def regroup(value):
            total = jnp.zeros((8, 128), F32)
            for k in range(8):
                moved = jnp.take_along_axis(
                    jnp.broadcast_to(value[k : k + 1, :], (8, 128)), pick, axis=1
                )
                total = jnp.where(k_here == k, moved, total)
            return total

        x, y, z = (regroup(part / floored) for part in (x, y, z))
        harmonic = [
            ROOT_THREE * x,
            ROOT_THREE * y,
            ROOT_THREE * z,
            ROOT_FIFTEEN * x * y,
            ROOT_FIFTEEN * y * z,
            ROOT_FIFTEEN * z * x,
            0.5 * ROOT_FIVE * (3.0 * z * z - 1.0),
            0.5 * ROOT_FIFTEEN * (x * x - y * y),
        ]
        diagonal = (lax.broadcasted_iota(jnp.int32, (32, 128), 1) & 31) == (
            lax.broadcasted_iota(jnp.int32, (32, 128), 0)
        )
        for m in range(8):
            scaled = harmonic[m] * 8.0**-0.5
            for group in range(4):
                for part in range(2):
                    r = 2 * group + part
                    block = jnp.where(
                        diagonal, jnp.broadcast_to(scaled[r : r + 1, :], (32, 128)), 0.0
                    )
                    spread[b, group, pl.ds(32 * m, 32), pl.ds(128 * part, 128)] = block.astype(BF16)

    def pick_half(b, both, k):
        part = both[128 * k : 128 * (k + 1)]
        upper = jnp.broadcast_to(halves[b, :, k : k + 1], (128, 128)) > 0.5
        return jnp.where(upper, part[:, 128:], part[:, :128])

    def pair_up(pairs_of_bins):
        return jnp.concatenate(
            [jnp.concatenate([ext[first], ext[second]], axis=1) for first, second in pairs_of_bins],
            axis=0,
        )

    def out_copy(hy, hz):
        return pltpu.make_async_copy(
            result.at[0, hy, hz], out.at[0, hy, hz], input_sem.at[2 * hy + hz]
        )

    def gather_inner(b):
        hz = b % 2
        table = pair_up(
            [((dx, 1, hz + dz), (dx, 2, hz + dz)) for dx in range(3) for dz in range(3)]
        )
        both = jnp.dot(hot_in[b], table, preferred_element_type=F32)
        for k in range(8):
            gathered[b, pl.ds(128 * k, 128)] = pick_half(b, both, k)

    def gather_column(b):
        row = 3 * (b // 2)
        table = pair_up([((1, row, 1), (1, row, 2))])
        both = jnp.dot(hot_out[b, :, pl.ds(512, 128)], table, preferred_element_type=F32)
        for k in range(8):
            gathered[b, pl.ds(128 * k, 128)] += pick_half(b, both, k)

    def finish(b):
        hy, hz = b // 2, b % 2
        row = 3 * hy
        table = pair_up(
            [((0, row, hz + dz), (2, row, hz + dz)) for dz in range(3)]
            + [((1, row, 3 * hz), (1, row, 3 * hz))]
        )
        both = jnp.dot(hot_out[b, :, pl.ds(0, 512)], table, preferred_element_type=F32)
        theirs = jnp.concatenate(
            [gathered[b, pl.ds(128 * k, 128)] + pick_half(b, both, k) for k in range(8)], axis=0
        )
        first = radial[b, :, 0:128].astype(F32) * theirs
        total = first[0:128]
        for k in range(1, 8):
            total = total + first[128 * k : 128 * (k + 1)]
        scalar_part = (total * 8.0**-0.5).astype(BF16)
        vector = (radial[b, :, 128:256].astype(F32) * theirs).astype(BF16)
        tensor = (radial[b, :, 256:384].astype(F32) * theirs).astype(BF16)
        norms = [[], []]
        for group in range(4):
            for which, (product, first_m, last_m) in enumerate(((vector, 0, 3), (tensor, 3, 8))):
                part = jnp.concatenate(
                    [product[128 * k + 32 * group : 128 * k + 32 * group + 32] for k in range(8)],
                    axis=0,
                )
                amp = jnp.dot(
                    spread[b, group, pl.ds(32 * first_m, 32 * (last_m - first_m)), :],
                    part,
                    preferred_element_type=F32,
                )
                norm = None
                for m in range(last_m - first_m):
                    piece = amp[32 * m : 32 * (m + 1)]
                    norm = piece * piece if norm is None else norm + piece * piece
                norms[which].append(norm.astype(BF16))
        joined = jnp.concatenate(
            [
                ext[1, 1 + hy, 1 + hz],
                scalar_part,
                jnp.concatenate(norms[0], axis=0),
                jnp.concatenate(norms[1], axis=0),
            ],
            axis=1,
        )
        mixed = jnp.dot(joined, mix_weight[...], preferred_element_type=F32)
        live_slot = lax.broadcasted_iota(jnp.int32, (128, 128), 0) < counts[0, hy, hz]
        result[0, hy, hz] = jnp.where(live_slot, mixed, 0.0).astype(BF16)
        out_copy(hy, hz).start()

    def each_bin(body, hy=None):
        def step(b, carry):
            body(b if hy is None else 2 * hy + b)
            return carry

        lax.fori_loop(0, 4 if hy is None else 2, step, 0)

    def greet(barrier, device):
        pl.semaphore_signal(barrier, inc=1, device_id=device, device_id_type=MESH)

    half_y = size_y // 2
    upper = me_y // half_y
    in_half = lax.rem(me_y, half_y)
    at_edge = (in_half == 0) | (in_half == half_y - 1)
    first_far, second_far = at_edge & (upper == 0), at_edge & (upper == 1)
    idle_above = size_z - 1 - z_last

    def between(pair):
        low = pair < idle_above
        y_first = jnp.where(upper == 0, me_y, lax.rem(me_y + far_step + size_y, size_y))
        return (
            me_x,
            jnp.where(low, y_first, y_first + half_y),
            jnp.where(low, z_last + 1 + pair, pair - idle_above),
        )

    @pl.when(jnp.logical_not(live))
    def _():
        result[...] = jnp.zeros_like(result)
        copy = pltpu.make_async_copy(result, out, own_sem)
        copy.start()
        low = (upper == 0) & (me_z > z_last)
        high = (upper == 1) & (me_z < z_first)

        @pl.when(at_edge & (low | high))
        def _():
            barrier = pltpu.get_barrier_semaphore()
            pair = jnp.where(low, me_z - z_last - 1, me_z + idle_above)
            pl.semaphore_wait(barrier, 2)
            pl.semaphore_signal(
                far_sem,
                inc=1,
                device_id=(me_x, me_y - half_y * upper, z_first + pair),
                device_id_type=MESH,
            )

        copy.wait()

    @pl.when(live)
    def _():
        barrier = pltpu.get_barrier_semaphore()
        pl.when(at_edge)(lambda: greet(barrier, between(me_z - z_first)))
        pl.when(jnp.logical_not(second_far))(lambda: greet(barrier, at(0, far_step, 0)))
        greet(barrier, at(0, -far_step, 0))
        for dx, dz in AROUND:
            pl.when(has(dz))(functools.partial(greet, barrier, at(dx, 0, dz)))

        inputs = [
            pltpu.make_async_copy(source, target, input_sem.at[n])
            for n, (source, target) in enumerate(
                (
                    (offs_in, offs),
                    (lists_in, lists),
                    (pairs_in, pairs),
                    (radial_in_in, radial_in),
                    (radial_out_in, radial_out),
                    (mix_weight_in, mix_weight),
                )
            )
        ]
        own_copy = pltpu.make_async_copy(feats.at[0], ext.at[1, pl.ds(1, 2), pl.ds(1, 2)], own_sem)
        own_copy.start()
        for copy in inputs:
            copy.start()
        inputs[0].wait()
        for y in range(2):
            for c in range(3):
                value = offs[0, y, c].astype(F32)
                for z in range(2):
                    places[1, 1, 1 + y, 3 * z + c : 3 * z + c + 1, :] = value[z : z + 1]
            places[1, 1, 1 + y, 6:8, :] = jnp.zeros((2, 128), F32)
        own_copy.wait()
        near = 3 + 3 * below.astype(jnp.int32) + 3 * above.astype(jnp.int32)
        pl.semaphore_wait(barrier, near + jnp.where(first_far, 0, 1))

        def send_far():
            place_y(late).start()
            for copy in feat_far(late):
                copy.start()

        def greeted():
            pl.semaphore_wait(far_sem, 1)
            send_far()

        pl.when(jnp.logical_not(first_far))(send_far)
        place_y(early).start()
        feat_y(early).start()
        pl.when(jnp.logical_not(second_far))(lambda: start_around(feat_own()))

        @pl.when(jnp.logical_not(below))
        def _():
            ext[:, :, 0] = jnp.zeros((3, 4, 128, 128), BF16)

        @pl.when(jnp.logical_not(above))
        def _():
            ext[:, :, 3] = jnp.zeros((3, 4, 128, 128), BF16)

        for copy in inputs[1:]:
            copy.wait()
        each_bin(one_hots)

        @pl.when(second_far)
        def _():
            start_around(feat_own())

        place_y(1 - early).wait_recv()
        start_around(place_early())
        feat_y(1 - early).wait_recv()
        start_around(feat_early())
        recv_around(place_early())
        each_bin(geometry, early)
        recv_around(feat_own())
        each_bin(gather_inner)
        each_bin(gather_column, early)
        soon = me_z - z_first >= size_z // 4
        pl.when(first_far & soon)(greeted)
        recv_around(feat_early())
        each_bin(finish, early)
        pl.when(first_far & jnp.logical_not(soon))(greeted)
        place_y(1 - late).wait_recv()
        start_around(place_late())
        for z, copy in enumerate(feat_far(1 - late)):
            copy.wait_recv()
            for dz, onward in feat_late(z):
                pl.when(has(dz))(onward.start)
        each_bin(gather_column, late)
        recv_around(place_late())
        each_bin(geometry, late)
        for z in range(2):
            for dz, onward in feat_late(z):
                pl.when(has(-dz))(onward.wait_recv)
        each_bin(finish, late)
        place_y(0).wait_send()
        place_y(1).wait_send()
        feat_y(early).wait_send()
        for copy in feat_far(late):
            copy.wait_send()
        for copies in (place_early, place_late, feat_own, feat_early):
            send_around(copies())
        for z in range(2):
            for dz, onward in feat_late(z):
                pl.when(has(dz))(onward.wait_send)
        for b in range(4):
            out_copy(b // 2, b % 2).wait()


def per_device(sizes, *arrays):
    node_feats, offsets, counts, neighbours, pair_counts, radial_in, radial_out, mix_weight = arrays
    hbm = pl.BlockSpec(memory_space=pl.ANY)
    return pl.pallas_call(
        functools.partial(kernel, sizes),
        out_shape=jax.ShapeDtypeStruct(node_feats.shape, BF16),
        in_specs=[hbm, hbm, hbm, hbm, pl.BlockSpec(memory_space=pltpu.SMEM), hbm, hbm, hbm],
        out_specs=hbm,
        scratch_shapes=[
            pltpu.VMEM((1, 2, 2, 128, 128), BF16),
            pltpu.VMEM((1, 2, 3, 2, 128), BF16),
            pltpu.VMEM((1, 2, 2, 8, 128), jnp.int32),
            pltpu.VMEM((1, 2, 2, 128), jnp.int32),
            pltpu.VMEM((8, 64), F32),
            pltpu.VMEM((64, 384), BF16),
            pltpu.VMEM((512, 128), BF16),
            pltpu.VMEM((3, 4, 4, 128, 128), BF16),
            pltpu.VMEM((3, 3, 4, 8, 128), F32),
            pltpu.VMEM((4, 1024, 1152), BF16),
            pltpu.VMEM((4, 1024, 640), BF16),
            pltpu.VMEM((4, 128, 8), F32),
            pltpu.VMEM((4, 4, 256, 256), BF16),
            pltpu.VMEM((4, 1024, 384), BF16),
            pltpu.VMEM((4, 1024, 128), F32),
            pltpu.SemaphoreType.DMA,
            pltpu.SemaphoreType.DMA((6,)),
            pltpu.SemaphoreType.DMA((48,)),
            pltpu.SemaphoreType.DMA((48,)),
            pltpu.SemaphoreType.REGULAR,
        ],
        compiler_params=pltpu.CompilerParams(
            collective_id=0, has_side_effects=True, vmem_limit_bytes=63 * 1024 * 1024
        ),
        cost_estimate=pl.CostEstimate(
            flops=4_000_000_000, bytes_accessed=4_000_000, transcendentals=600_000
        ),
    )(
        node_feats,
        jnp.transpose(offsets, (0, 1, 3, 2, 4)),
        jnp.swapaxes(neighbours, 3, 4),
        pair_counts,
        counts,
        radial_in,
        radial_out,
        mix_weight,
    )


def solution(mesh):
    placed = (
        P("gx", "gy", "gz", None, None),
        P("gx", "gy", "gz", None, None),
        P("gx", "gy", "gz"),
        P("gx", "gy", "gz", None, None),
        P("gx", "gy", "gz", None),
        P(),
        P(),
        P(),
    )
    sizes = tuple(mesh.shape[axis] for axis in AXES)
    return jax.shard_map(
        functools.partial(per_device, sizes),
        mesh=mesh,
        in_specs=placed,
        out_specs=P("gx", "gy", "gz", None, None),
        check_vma=False,
    )
```

```python
import functools
import math

import jax
import jax.numpy as jnp
from jax import lax
from jax.experimental import pallas as pl
from jax.experimental.pallas import tpu as pltpu
from jax.sharding import PartitionSpec as P

ROOT_THREE = math.sqrt(3.0)
ROOT_FIVE = math.sqrt(5.0)
ROOT_FIFTEEN = math.sqrt(15.0)
CUTOFF_BINS = 3.0
FLOOR_BINS = 0.25
AXES = ("gx", "gy", "gz")
MESH = pl.DeviceIdType.MESH
AROUND = [(-1, -1), (1, -1), (-1, 1), (1, 1), (0, -1), (0, 1), (-1, 0), (1, 0)]
BF16 = jnp.bfloat16
F32 = jnp.float32


def sin_pi(value):
    whole = jnp.floor(value + 0.5)
    r = value - whole
    odd = whole - 2.0 * jnp.floor(0.5 * whole)
    square = r * r
    total = jnp.full_like(r, -(math.pi**11) / math.factorial(11))
    for power in (9, 7, 5, 3, 1):
        sign = 1.0 if power % 4 == 1 else -1.0
        total = total * square + sign * math.pi**power / math.factorial(power)
    return (1.0 - 2.0 * odd) * r * total


def kernel(
    sizes,
    feats,
    offs_in,
    lists_in,
    pairs_in,
    counts,
    radial_in_in,
    radial_out_in,
    mix_weight_in,
    out,
    result,
    offs,
    lists,
    pairs,
    radial_in,
    radial_out,
    mix_weight,
    ext,
    places,
    hot_in,
    hot_out,
    halves,
    spread,
    radial,
    gathered,
    own_sem,
    input_sem,
    send_sem,
    recv_sem,
    far_sem,
):
    size_x, size_y, size_z = sizes
    me_x, me_y, me_z = (lax.axis_index(axis) for axis in AXES)
    z_first, z_last = size_z // 4, size_z // 4 + size_z // 2 - 1
    live = (me_z >= z_first) & (me_z <= z_last)
    below, above = me_z > z_first, me_z < z_last

    def has(dz):
        return {-1: below, 0: me_z >= 0, 1: above}[dz]

    def at(dx, dy, dz):
        return (
            lax.rem(me_x + dx + size_x, size_x),
            lax.rem(me_y + dy + size_y, size_y),
            lax.rem(me_z + dz + size_z, size_z),
        )

    def remote(number, source, target, device):
        return pltpu.make_async_remote_copy(
            src_ref=source,
            dst_ref=target,
            send_sem=send_sem.at[number],
            recv_sem=recv_sem.at[number],
            device_id=device,
            device_id_type=MESH,
        )

    z_from = {-1: pl.ds(1, 1), 0: pl.ds(1, 2), 1: pl.ds(2, 1)}
    z_to = {-1: pl.ds(3, 1), 0: pl.ds(1, 2), 1: pl.ds(0, 1)}

    late = lax.rem(me_y, 2)
    early = 1 - late
    far_step = 2 * late - 1

    def to_y(first, source, target, slot):
        return remote(first + slot, source, target, at(0, 2 * slot - 1, 0))

    def place_y(slot):
        return to_y(0, places.at[1, 1, 1 + slot], places.at[1, 1, 3 - 3 * slot], slot)

    def feat_y(slot):
        return to_y(
            2, ext.at[1, 1 + slot, pl.ds(1, 2)], ext.at[1, 3 - 3 * slot, pl.ds(1, 2)], slot
        )

    def around(first, source, target):
        return [
            remote(first + n, source(dx, dz), target(dx, dz), at(dx, 0, dz))
            for n, (dx, dz) in enumerate(AROUND)
        ]

    def place_early():
        rows = pl.ds(early, 3)
        return around(
            4,
            lambda dx, dz: places.at[1, 1, rows],
            lambda dx, dz: places.at[1 - dx, 1 - dz, rows],
        )

    def place_late():
        return around(
            12,
            lambda dx, dz: places.at[1, 1, 3 * late],
            lambda dx, dz: places.at[1 - dx, 1 - dz, 3 * late],
        )

    def feat_own():
        return around(
            20,
            lambda dx, dz: ext.at[1, pl.ds(1, 2), z_from[dz]],
            lambda dx, dz: ext.at[1 - dx, pl.ds(1, 2), z_to[dz]],
        )

    def feat_relay(first, row):
        return around(
            first,
            lambda dx, dz: ext.at[1, row, z_from[dz]],
            lambda dx, dz: ext.at[1 - dx, row, z_to[dz]],
        )

    def feat_early():
        return feat_relay(28, 3 * early)

    def feat_late():
        return feat_relay(36, 3 * late)

    def start_around(copies):
        for (dx, dz), copy in zip(AROUND, copies):
            pl.when(has(dz))(copy.start)

    def recv_around(copies):
        for (dx, dz), copy in zip(AROUND, copies):
            pl.when(has(-dz))(copy.wait_recv)

    def send_around(copies):
        for (dx, dz), copy in zip(AROUND, copies):
            pl.when(has(dz))(copy.wait_send)

    def lists_of(b):
        hy, hz = b // 2, b % 2
        flat = lists[0, hy, hz]
        digit = flat >> 7
        step_x = (digit * 57) >> 9
        rest = digit - 9 * step_x
        step_y = (rest * 11) >> 5
        step_z = rest - 3 * step_y
        return flat & 127, digit, step_x, step_y, step_z

    lane = lax.broadcasted_iota(jnp.int32, (8, 128), 1)
    row = lax.broadcasted_iota(jnp.int32, (8, 128), 0)

    def one_hots(b):
        hy, hz = b // 2, b % 2
        slot, _, step_x, step_y, step_z = lists_of(b)
        used = row < pairs[0, hy, pl.ds(hz, 1), :]
        layer = step_y - 1 + hy
        inner = (layer == 0) | (layer == 1)
        around = step_x * 3 + step_z
        t_in = jnp.where(used & inner, around, -1)
        column = step_x == 1
        beyond = column & (step_z == 2 * hz)
        chunk = jnp.where(column, jnp.where(beyond, 3, 4), step_z)
        t_out = jnp.where(used & jnp.logical_not(inner), chunk, -1)
        side = jnp.where(column, jnp.where(beyond, 0, step_z - 1 + hz), step_x >> 1)
        slot_col = slot.astype(F32).T
        in_col = t_in.astype(F32).T
        out_col = t_out.astype(F32).T
        halves[b] = jnp.where(inner, layer, side).astype(F32).T
        lanes = lax.broadcasted_iota(jnp.int32, (128, 128), 1).astype(F32).astype(BF16)
        zero = jnp.zeros((128, 128), BF16)
        for k in range(8):
            rows = pl.ds(128 * k, 128)

            def spread_col(col):
                return jnp.broadcast_to(col[:, k : k + 1], (128, 128)).astype(BF16)

            slots = jnp.where(spread_col(slot_col) == lanes, jnp.ones_like(zero), zero)
            in_k, out_k = spread_col(in_col), spread_col(out_col)
            for t in range(9):
                cols = pl.ds(128 * t, 128)
                hot_in[b, rows, cols] = jnp.where(in_k == float(t), slots, zero)
                if t < 5:
                    hot_out[b, rows, cols] = jnp.where(out_k == float(t), slots, zero)

    def geometry(b):
        hy, hz = b // 2, b % 2
        slot, digit, step_x, step_y, step_z = lists_of(b)
        theirs = [jnp.zeros((8, 128), F32) for _ in range(3)]
        for d in range(27):
            dx, dy, dz = d // 9, d // 3 % 3, d % 3
            there = hz + dz
            chosen = digit == d
            for c in range(3):
                table = places[dx, (there + 1) // 2, hy + dy, pl.ds((there + 1) % 2 * 3 + c, 1), :]
                value = jnp.take_along_axis(jnp.broadcast_to(table, (8, 128)), slot, axis=1)
                theirs[c] = jnp.where(chosen, value, theirs[c])
        displace = []
        for c, step in enumerate((step_x, step_y, step_z)):
            own = places[1, 1, 1 + hy, pl.ds(hz * 3 + c, 1), :]
            displace.append((step - 1).astype(F32) + theirs[c] - own)
        x, y, z = displace
        distance = jnp.sqrt(x * x + y * y + z * z)
        floored = jnp.maximum(distance, FLOOR_BINS)
        u = jnp.minimum(distance / CUTOFF_BINS, 1.0)
        cube = u * u * u
        envelope = 1.0 - 10.0 * cube + 15.0 * cube * u - 6.0 * cube * u * u
        height = envelope / floored

        def along(value):
            return jnp.concatenate(
                [jnp.broadcast_to(value[k : k + 1, :], (8, 128)) for k in range(8)], axis=1
            )

        order = (lax.broadcasted_iota(jnp.int32, (8, 1024), 0) + 1).astype(F32)
        basis = sin_pi(order * along(u)) * along(height)
        before = jnp.dot(
            radial_in[...].T, basis, precision=lax.Precision.HIGHEST, preferred_element_type=F32
        )
        hidden = (0.5 * before * (1.0 + jnp.tanh(0.5 * before))).T.astype(BF16)
        radial[b] = jnp.dot(hidden, radial_out[...], preferred_element_type=F32).astype(BF16)

        pick = (row >> 1) * 32 + (lane & 31)
        k_here = (row & 1) * 4 + (lane >> 5)

        def regroup(value):
            total = jnp.zeros((8, 128), F32)
            for k in range(8):
                moved = jnp.take_along_axis(
                    jnp.broadcast_to(value[k : k + 1, :], (8, 128)), pick, axis=1
                )
                total = jnp.where(k_here == k, moved, total)
            return total

        x, y, z = (regroup(part / floored) for part in (x, y, z))
        harmonic = [
            ROOT_THREE * x,
            ROOT_THREE * y,
            ROOT_THREE * z,
            ROOT_FIFTEEN * x * y,
            ROOT_FIFTEEN * y * z,
            ROOT_FIFTEEN * z * x,
            0.5 * ROOT_FIVE * (3.0 * z * z - 1.0),
            0.5 * ROOT_FIFTEEN * (x * x - y * y),
        ]
        diagonal = (lax.broadcasted_iota(jnp.int32, (32, 128), 1) & 31) == (
            lax.broadcasted_iota(jnp.int32, (32, 128), 0)
        )
        for m in range(8):
            scaled = harmonic[m] * 8.0**-0.5
            for group in range(4):
                for part in range(2):
                    r = 2 * group + part
                    block = jnp.where(
                        diagonal, jnp.broadcast_to(scaled[r : r + 1, :], (32, 128)), 0.0
                    )
                    spread[b, group, pl.ds(32 * m, 32), pl.ds(128 * part, 128)] = block.astype(BF16)

    def pick_half(b, both, k):
        part = both[128 * k : 128 * (k + 1)]
        upper = jnp.broadcast_to(halves[b, :, k : k + 1], (128, 128)) > 0.5
        return jnp.where(upper, part[:, 128:], part[:, :128])

    def pair_up(pairs_of_bins):
        return jnp.concatenate(
            [jnp.concatenate([ext[first], ext[second]], axis=1) for first, second in pairs_of_bins],
            axis=0,
        )

    def out_copy(hy, hz):
        return pltpu.make_async_copy(
            result.at[0, hy, hz], out.at[0, hy, hz], input_sem.at[2 * hy + hz]
        )

    def gather_inner(b):
        hz = b % 2
        table = pair_up(
            [((dx, 1, hz + dz), (dx, 2, hz + dz)) for dx in range(3) for dz in range(3)]
        )
        both = jnp.dot(hot_in[b], table, preferred_element_type=F32)
        for k in range(8):
            gathered[b, pl.ds(128 * k, 128)] = pick_half(b, both, k)

    def gather_column(b):
        row = 3 * (b // 2)
        table = pair_up([((1, row, 1), (1, row, 2))])
        both = jnp.dot(hot_out[b, :, pl.ds(512, 128)], table, preferred_element_type=F32)
        for k in range(8):
            gathered[b, pl.ds(128 * k, 128)] += pick_half(b, both, k)

    def finish(b):
        hy, hz = b // 2, b % 2
        row = 3 * hy
        table = pair_up(
            [((0, row, hz + dz), (2, row, hz + dz)) for dz in range(3)]
            + [((1, row, 3 * hz), (1, row, 3 * hz))]
        )
        both = jnp.dot(hot_out[b, :, pl.ds(0, 512)], table, preferred_element_type=F32)
        theirs = jnp.concatenate(
            [gathered[b, pl.ds(128 * k, 128)] + pick_half(b, both, k) for k in range(8)], axis=0
        )
        first = radial[b, :, 0:128].astype(F32) * theirs
        total = first[0:128]
        for k in range(1, 8):
            total = total + first[128 * k : 128 * (k + 1)]
        scalar_part = (total * 8.0**-0.5).astype(BF16)
        vector = (radial[b, :, 128:256].astype(F32) * theirs).astype(BF16)
        tensor = (radial[b, :, 256:384].astype(F32) * theirs).astype(BF16)
        norms = [[], []]
        for group in range(4):
            for which, (product, first_m, last_m) in enumerate(((vector, 0, 3), (tensor, 3, 8))):
                part = jnp.concatenate(
                    [product[128 * k + 32 * group : 128 * k + 32 * group + 32] for k in range(8)],
                    axis=0,
                )
                amp = jnp.dot(
                    spread[b, group, pl.ds(32 * first_m, 32 * (last_m - first_m)), :],
                    part,
                    preferred_element_type=F32,
                )
                norm = None
                for m in range(last_m - first_m):
                    piece = amp[32 * m : 32 * (m + 1)]
                    norm = piece * piece if norm is None else norm + piece * piece
                norms[which].append(norm.astype(BF16))
        joined = jnp.concatenate(
            [
                ext[1, 1 + hy, 1 + hz],
                scalar_part,
                jnp.concatenate(norms[0], axis=0),
                jnp.concatenate(norms[1], axis=0),
            ],
            axis=1,
        )
        mixed = jnp.dot(joined, mix_weight[...], preferred_element_type=F32)
        live_slot = lax.broadcasted_iota(jnp.int32, (128, 128), 0) < counts[0, hy, hz]
        result[0, hy, hz] = jnp.where(live_slot, mixed, 0.0).astype(BF16)
        out_copy(hy, hz).start()

    def each_bin(body, hy=None):
        def step(b, carry):
            body(b if hy is None else 2 * hy + b)
            return carry

        lax.fori_loop(0, 4 if hy is None else 2, step, 0)

    def greet(barrier, device):
        pl.semaphore_signal(barrier, inc=1, device_id=device, device_id_type=MESH)

    half_y = size_y // 2
    upper = me_y // half_y
    in_half = lax.rem(me_y, half_y)
    at_edge = (in_half == 0) | (in_half == half_y - 1)
    first_far, second_far = at_edge & (upper == 0), at_edge & (upper == 1)
    idle_above = size_z - 1 - z_last

    def between(pair):
        low = pair < idle_above
        y_first = jnp.where(upper == 0, me_y, lax.rem(me_y + far_step + size_y, size_y))
        return (
            me_x,
            jnp.where(low, y_first, y_first + half_y),
            jnp.where(low, z_last + 1 + pair, pair - idle_above),
        )

    @pl.when(jnp.logical_not(live))
    def _():
        result[...] = jnp.zeros_like(result)
        copy = pltpu.make_async_copy(result, out, own_sem)
        copy.start()
        low = (upper == 0) & (me_z > z_last)
        high = (upper == 1) & (me_z < z_first)

        @pl.when(at_edge & (low | high))
        def _():
            barrier = pltpu.get_barrier_semaphore()
            pair = jnp.where(low, me_z - z_last - 1, me_z + idle_above)
            pl.semaphore_wait(barrier, 2)
            pl.semaphore_signal(
                far_sem,
                inc=1,
                device_id=(me_x, me_y - half_y * upper, z_first + pair),
                device_id_type=MESH,
            )

        copy.wait()

    @pl.when(live)
    def _():
        barrier = pltpu.get_barrier_semaphore()
        pl.when(at_edge)(lambda: greet(barrier, between(me_z - z_first)))
        pl.when(jnp.logical_not(second_far))(lambda: greet(barrier, at(0, far_step, 0)))
        greet(barrier, at(0, -far_step, 0))
        for dx, dz in AROUND:
            pl.when(has(dz))(functools.partial(greet, barrier, at(dx, 0, dz)))

        inputs = [
            pltpu.make_async_copy(source, target, input_sem.at[n])
            for n, (source, target) in enumerate(
                (
                    (offs_in, offs),
                    (lists_in, lists),
                    (pairs_in, pairs),
                    (radial_in_in, radial_in),
                    (radial_out_in, radial_out),
                    (mix_weight_in, mix_weight),
                )
            )
        ]
        own_copy = pltpu.make_async_copy(feats.at[0], ext.at[1, pl.ds(1, 2), pl.ds(1, 2)], own_sem)
        own_copy.start()
        for copy in inputs:
            copy.start()
        inputs[0].wait()
        for y in range(2):
            for c in range(3):
                value = offs[0, y, c].astype(F32)
                for z in range(2):
                    places[1, 1, 1 + y, 3 * z + c : 3 * z + c + 1, :] = value[z : z + 1]
            places[1, 1, 1 + y, 6:8, :] = jnp.zeros((2, 128), F32)
        own_copy.wait()
        near = 3 + 3 * below.astype(jnp.int32) + 3 * above.astype(jnp.int32)
        pl.semaphore_wait(barrier, near + jnp.where(first_far, 0, 1))

        def send_far():
            place_y(late).start()
            feat_y(late).start()

        def greeted():
            pl.semaphore_wait(far_sem, 1)
            send_far()

        pl.when(jnp.logical_not(first_far))(send_far)
        place_y(early).start()
        feat_y(early).start()
        pl.when(jnp.logical_not(second_far))(lambda: start_around(feat_own()))

        @pl.when(jnp.logical_not(below))
        def _():
            ext[:, :, 0] = jnp.zeros((3, 4, 128, 128), BF16)

        @pl.when(jnp.logical_not(above))
        def _():
            ext[:, :, 3] = jnp.zeros((3, 4, 128, 128), BF16)

        for copy in inputs[1:]:
            copy.wait()
        each_bin(one_hots)

        @pl.when(second_far)
        def _():
            start_around(feat_own())

        place_y(1 - early).wait_recv()
        start_around(place_early())
        feat_y(1 - early).wait_recv()
        start_around(feat_early())
        recv_around(place_early())
        each_bin(geometry, early)
        recv_around(feat_own())
        each_bin(gather_inner)
        each_bin(gather_column, early)
        soon = me_z - z_first >= size_z // 4
        pl.when(first_far & soon)(greeted)
        recv_around(feat_early())
        each_bin(finish, early)
        pl.when(first_far & jnp.logical_not(soon))(greeted)
        place_y(early).wait_send()
        feat_y(early).wait_send()
        for copies in (place_early, feat_own, feat_early):
            send_around(copies())
        place_y(1 - late).wait_recv()
        start_around(place_late())
        feat_y(1 - late).wait_recv()
        start_around(feat_late())
        each_bin(gather_column, late)
        first_hz = jnp.where(above, 0, 1)

        def recv_from(copies, step, also):
            for (_, dz), copy in zip(AROUND, copies()):
                if dz == step:
                    pl.when(has(-dz) & also)(copy.wait_recv)

        def recv_first(copies):
            recv_from(copies, 0, live)
            recv_from(copies, 1, above)

        def recv_second(copies):
            recv_from(copies, 1, jnp.logical_not(above))
            recv_from(copies, -1, live)

        def last_bins(t, carry):
            b = 2 * late + jnp.where(t == 0, first_hz, 1 - first_hz)
            pl.when(t == 0)(lambda: recv_first(place_late))
            pl.when(t == 1)(lambda: recv_second(place_late))
            geometry(b)
            pl.when(t == 0)(lambda: recv_first(feat_late))

            @pl.when(t == 1)
            def _():
                place_y(late).wait_send()
                feat_y(late).wait_send()
                send_around(place_late())
                recv_second(feat_late)
                send_around(feat_late())

            finish(b)
            return carry

        lax.fori_loop(0, 2, last_bins, 0)
        for b in range(4):
            out_copy(b // 2, b % 2).wait()


def per_device(sizes, *arrays):
    node_feats, offsets, counts, neighbours, pair_counts, radial_in, radial_out, mix_weight = arrays
    hbm = pl.BlockSpec(memory_space=pl.ANY)
    return pl.pallas_call(
        functools.partial(kernel, sizes),
        out_shape=jax.ShapeDtypeStruct(node_feats.shape, BF16),
        in_specs=[hbm, hbm, hbm, hbm, pl.BlockSpec(memory_space=pltpu.SMEM), hbm, hbm, hbm],
        out_specs=hbm,
        scratch_shapes=[
            pltpu.VMEM((1, 2, 2, 128, 128), BF16),
            pltpu.VMEM((1, 2, 3, 2, 128), BF16),
            pltpu.VMEM((1, 2, 2, 8, 128), jnp.int32),
            pltpu.VMEM((1, 2, 2, 128), jnp.int32),
            pltpu.VMEM((8, 64), F32),
            pltpu.VMEM((64, 384), BF16),
            pltpu.VMEM((512, 128), BF16),
            pltpu.VMEM((3, 4, 4, 128, 128), BF16),
            pltpu.VMEM((3, 3, 4, 8, 128), F32),
            pltpu.VMEM((4, 1024, 1152), BF16),
            pltpu.VMEM((4, 1024, 640), BF16),
            pltpu.VMEM((4, 128, 8), F32),
            pltpu.VMEM((4, 4, 256, 256), BF16),
            pltpu.VMEM((4, 1024, 384), BF16),
            pltpu.VMEM((4, 1024, 128), F32),
            pltpu.SemaphoreType.DMA,
            pltpu.SemaphoreType.DMA((6,)),
            pltpu.SemaphoreType.DMA((44,)),
            pltpu.SemaphoreType.DMA((44,)),
            pltpu.SemaphoreType.REGULAR,
        ],
        compiler_params=pltpu.CompilerParams(
            collective_id=0, has_side_effects=True, vmem_limit_bytes=63 * 1024 * 1024
        ),
        cost_estimate=pl.CostEstimate(
            flops=4_000_000_000, bytes_accessed=4_000_000, transcendentals=600_000
        ),
    )(
        node_feats,
        jnp.transpose(offsets, (0, 1, 3, 2, 4)),
        jnp.swapaxes(neighbours, 3, 4),
        pair_counts,
        counts,
        radial_in,
        radial_out,
        mix_weight,
    )


def solution(mesh):
    placed = (
        P("gx", "gy", "gz", None, None),
        P("gx", "gy", "gz", None, None),
        P("gx", "gy", "gz"),
        P("gx", "gy", "gz", None, None),
        P("gx", "gy", "gz", None),
        P(),
        P(),
        P(),
    )
    sizes = tuple(mesh.shape[axis] for axis in AXES)
    return jax.shard_map(
        functools.partial(per_device, sizes),
        mesh=mesh,
        in_specs=placed,
        out_specs=P("gx", "gy", "gz", None, None),
        check_vma=False,
    )
```

```python
import functools
import math

import jax
import jax.numpy as jnp
from jax import lax
from jax.experimental import pallas as pl
from jax.experimental.pallas import tpu as pltpu
from jax.sharding import PartitionSpec as P

ROOT_THREE = math.sqrt(3.0)
ROOT_FIVE = math.sqrt(5.0)
ROOT_FIFTEEN = math.sqrt(15.0)
CUTOFF_BINS = 3.0
FLOOR_BINS = 0.25
AXES = ("gx", "gy", "gz")
MESH = pl.DeviceIdType.MESH
AROUND = [(-1, -1), (1, -1), (-1, 1), (1, 1), (0, -1), (0, 1), (-1, 0), (1, 0)]
BF16 = jnp.bfloat16
F32 = jnp.float32


def sin_pi(value):
    whole = jnp.floor(value + 0.5)
    r = value - whole
    odd = whole - 2.0 * jnp.floor(0.5 * whole)
    square = r * r
    total = jnp.full_like(r, -(math.pi**11) / math.factorial(11))
    for power in (9, 7, 5, 3, 1):
        sign = 1.0 if power % 4 == 1 else -1.0
        total = total * square + sign * math.pi**power / math.factorial(power)
    return (1.0 - 2.0 * odd) * r * total


def kernel(
    sizes,
    feats,
    offs_in,
    lists_in,
    pairs_in,
    counts,
    radial_in_in,
    radial_out_in,
    mix_weight_in,
    out,
    offs,
    lists,
    pairs,
    radial_in,
    radial_out,
    mix_weight,
    ext,
    places,
    hot_in,
    hot_out,
    halves,
    spread,
    radial,
    gathered,
    own_sem,
    input_sem,
    send_sem,
    recv_sem,
    far_sem,
):
    size_x, size_y, size_z = sizes
    me_x, me_y, me_z = (lax.axis_index(axis) for axis in AXES)
    z_first, z_last = size_z // 4, size_z // 4 + size_z // 2 - 1
    live = (me_z >= z_first) & (me_z <= z_last)
    below, above = me_z > z_first, me_z < z_last

    def has(dz):
        return {-1: below, 0: me_z >= 0, 1: above}[dz]

    def at(dx, dy, dz):
        return (
            lax.rem(me_x + dx + size_x, size_x),
            lax.rem(me_y + dy + size_y, size_y),
            lax.rem(me_z + dz + size_z, size_z),
        )

    def remote(number, source, target, device):
        return pltpu.make_async_remote_copy(
            src_ref=source,
            dst_ref=target,
            send_sem=send_sem.at[number],
            recv_sem=recv_sem.at[number],
            device_id=device,
            device_id_type=MESH,
        )

    z_from = {-1: pl.ds(1, 1), 0: pl.ds(1, 2), 1: pl.ds(2, 1)}
    z_to = {-1: pl.ds(3, 1), 0: pl.ds(1, 2), 1: pl.ds(0, 1)}

    late = lax.rem(me_y, 2)
    early = 1 - late
    far_step = 2 * late - 1

    def to_y(first, source, target, slot):
        return remote(first + slot, source, target, at(0, 2 * slot - 1, 0))

    def place_y(slot):
        return to_y(0, places.at[1, 1, 1 + slot], places.at[1, 1, 3 - 3 * slot], slot)

    def feat_y(slot):
        return to_y(
            2, ext.at[1, 1 + slot, pl.ds(1, 2)], ext.at[1, 3 - 3 * slot, pl.ds(1, 2)], slot
        )

    def around(first, source, target):
        return [
            remote(first + n, source(dx, dz), target(dx, dz), at(dx, 0, dz))
            for n, (dx, dz) in enumerate(AROUND)
        ]

    def place_early():
        rows = pl.ds(early, 3)
        return around(
            4,
            lambda dx, dz: places.at[1, 1, rows],
            lambda dx, dz: places.at[1 - dx, 1 - dz, rows],
        )

    def place_late():
        return around(
            12,
            lambda dx, dz: places.at[1, 1, 3 * late],
            lambda dx, dz: places.at[1 - dx, 1 - dz, 3 * late],
        )

    def feat_own():
        return around(
            20,
            lambda dx, dz: ext.at[1, pl.ds(1, 2), z_from[dz]],
            lambda dx, dz: ext.at[1 - dx, pl.ds(1, 2), z_to[dz]],
        )

    def feat_relay(first, row):
        return around(
            first,
            lambda dx, dz: ext.at[1, row, z_from[dz]],
            lambda dx, dz: ext.at[1 - dx, row, z_to[dz]],
        )

    def feat_early():
        return feat_relay(28, 3 * early)

    def feat_late():
        return feat_relay(36, 3 * late)

    def start_around(copies):
        for (dx, dz), copy in zip(AROUND, copies):
            pl.when(has(dz))(copy.start)

    def recv_around(copies):
        for (dx, dz), copy in zip(AROUND, copies):
            pl.when(has(-dz))(copy.wait_recv)

    def send_around(copies):
        for (dx, dz), copy in zip(AROUND, copies):
            pl.when(has(dz))(copy.wait_send)

    def lists_of(b):
        hy, hz = b // 2, b % 2
        flat = lists[0, hy, hz]
        digit = flat >> 7
        step_x = (digit * 57) >> 9
        rest = digit - 9 * step_x
        step_y = (rest * 11) >> 5
        step_z = rest - 3 * step_y
        return flat & 127, digit, step_x, step_y, step_z

    lane = lax.broadcasted_iota(jnp.int32, (8, 128), 1)
    row = lax.broadcasted_iota(jnp.int32, (8, 128), 0)

    def one_hots(b):
        hy, hz = b // 2, b % 2
        slot, _, step_x, step_y, step_z = lists_of(b)
        used = row < pairs[0, hy, pl.ds(hz, 1), :]
        layer = step_y - 1 + hy
        inner = (layer == 0) | (layer == 1)
        around = step_x * 3 + step_z
        t_in = jnp.where(used & inner, around, -1)
        column = step_x == 1
        beyond = column & (step_z == 2 * hz)
        chunk = jnp.where(column, jnp.where(beyond, 3, 4), step_z)
        t_out = jnp.where(used & jnp.logical_not(inner), chunk, -1)
        side = jnp.where(column, jnp.where(beyond, 0, step_z - 1 + hz), step_x >> 1)
        slot_col = slot.astype(F32).T
        in_col = t_in.astype(F32).T
        out_col = t_out.astype(F32).T
        halves[b] = jnp.where(inner, layer, side).astype(F32).T
        lanes = lax.broadcasted_iota(jnp.int32, (128, 128), 1).astype(F32).astype(BF16)
        zero = jnp.zeros((128, 128), BF16)
        for k in range(8):
            rows = pl.ds(128 * k, 128)

            def spread_col(col):
                return jnp.broadcast_to(col[:, k : k + 1], (128, 128)).astype(BF16)

            slots = jnp.where(spread_col(slot_col) == lanes, jnp.ones_like(zero), zero)
            in_k, out_k = spread_col(in_col), spread_col(out_col)
            for t in range(9):
                cols = pl.ds(128 * t, 128)
                hot_in[b, rows, cols] = jnp.where(in_k == float(t), slots, zero)
                if t < 5:
                    hot_out[b, rows, cols] = jnp.where(out_k == float(t), slots, zero)

    def geometry(b):
        hy, hz = b // 2, b % 2
        slot, digit, step_x, step_y, step_z = lists_of(b)
        theirs = [jnp.zeros((8, 128), F32) for _ in range(3)]
        for d in range(27):
            dx, dy, dz = d // 9, d // 3 % 3, d % 3
            there = hz + dz
            chosen = digit == d
            for c in range(3):
                table = places[dx, (there + 1) // 2, hy + dy, pl.ds((there + 1) % 2 * 3 + c, 1), :]
                value = jnp.take_along_axis(jnp.broadcast_to(table, (8, 128)), slot, axis=1)
                theirs[c] = jnp.where(chosen, value, theirs[c])
        displace = []
        for c, step in enumerate((step_x, step_y, step_z)):
            own = places[1, 1, 1 + hy, pl.ds(hz * 3 + c, 1), :]
            displace.append((step - 1).astype(F32) + theirs[c] - own)
        x, y, z = displace
        distance = jnp.sqrt(x * x + y * y + z * z)
        floored = jnp.maximum(distance, FLOOR_BINS)
        u = jnp.minimum(distance / CUTOFF_BINS, 1.0)
        cube = u * u * u
        envelope = 1.0 - 10.0 * cube + 15.0 * cube * u - 6.0 * cube * u * u
        height = envelope / floored

        def along(value):
            return jnp.concatenate(
                [jnp.broadcast_to(value[k : k + 1, :], (8, 128)) for k in range(8)], axis=1
            )

        order = (lax.broadcasted_iota(jnp.int32, (8, 1024), 0) + 1).astype(F32)
        basis = sin_pi(order * along(u)) * along(height)
        before = jnp.dot(
            radial_in[...].T, basis, precision=lax.Precision.HIGHEST, preferred_element_type=F32
        )
        hidden = (0.5 * before * (1.0 + jnp.tanh(0.5 * before))).T.astype(BF16)
        radial[b] = jnp.dot(hidden, radial_out[...], preferred_element_type=F32).astype(BF16)

        pick = (row >> 1) * 32 + (lane & 31)
        k_here = (row & 1) * 4 + (lane >> 5)

        def regroup(value):
            total = jnp.zeros((8, 128), F32)
            for k in range(8):
                moved = jnp.take_along_axis(
                    jnp.broadcast_to(value[k : k + 1, :], (8, 128)), pick, axis=1
                )
                total = jnp.where(k_here == k, moved, total)
            return total

        x, y, z = (regroup(part / floored) for part in (x, y, z))
        harmonic = [
            ROOT_THREE * x,
            ROOT_THREE * y,
            ROOT_THREE * z,
            ROOT_FIFTEEN * x * y,
            ROOT_FIFTEEN * y * z,
            ROOT_FIFTEEN * z * x,
            0.5 * ROOT_FIVE * (3.0 * z * z - 1.0),
            0.5 * ROOT_FIFTEEN * (x * x - y * y),
        ]
        diagonal = (lax.broadcasted_iota(jnp.int32, (32, 128), 1) & 31) == (
            lax.broadcasted_iota(jnp.int32, (32, 128), 0)
        )
        for m in range(8):
            scaled = harmonic[m] * 8.0**-0.5
            for group in range(4):
                for part in range(2):
                    r = 2 * group + part
                    block = jnp.where(
                        diagonal, jnp.broadcast_to(scaled[r : r + 1, :], (32, 128)), 0.0
                    )
                    spread[b, group, pl.ds(32 * m, 32), pl.ds(128 * part, 128)] = block.astype(BF16)

    def pick_half(b, both, k):
        part = both[128 * k : 128 * (k + 1)]
        upper = jnp.broadcast_to(halves[b, :, k : k + 1], (128, 128)) > 0.5
        return jnp.where(upper, part[:, 128:], part[:, :128])

    def pair_up(pairs_of_bins):
        return jnp.concatenate(
            [jnp.concatenate([ext[first], ext[second]], axis=1) for first, second in pairs_of_bins],
            axis=0,
        )

    def gather_inner(b):
        hz = b % 2
        table = pair_up(
            [((dx, 1, hz + dz), (dx, 2, hz + dz)) for dx in range(3) for dz in range(3)]
        )
        both = jnp.dot(hot_in[b], table, preferred_element_type=F32)
        for k in range(8):
            gathered[b, pl.ds(128 * k, 128)] = pick_half(b, both, k)

    def gather_column(b):
        row = 3 * (b // 2)
        table = pair_up([((1, row, 1), (1, row, 2))])
        both = jnp.dot(hot_out[b, :, pl.ds(512, 128)], table, preferred_element_type=F32)
        for k in range(8):
            gathered[b, pl.ds(128 * k, 128)] += pick_half(b, both, k)

    def finish(b):
        hy, hz = b // 2, b % 2
        row = 3 * hy
        table = pair_up(
            [((0, row, hz + dz), (2, row, hz + dz)) for dz in range(3)]
            + [((1, row, 3 * hz), (1, row, 3 * hz))]
        )
        both = jnp.dot(hot_out[b, :, pl.ds(0, 512)], table, preferred_element_type=F32)
        theirs = jnp.concatenate(
            [gathered[b, pl.ds(128 * k, 128)] + pick_half(b, both, k) for k in range(8)], axis=0
        )
        first = radial[b, :, 0:128].astype(F32) * theirs
        total = first[0:128]
        for k in range(1, 8):
            total = total + first[128 * k : 128 * (k + 1)]
        scalar_part = (total * 8.0**-0.5).astype(BF16)
        vector = (radial[b, :, 128:256].astype(F32) * theirs).astype(BF16)
        tensor = (radial[b, :, 256:384].astype(F32) * theirs).astype(BF16)
        norms = [[], []]
        for group in range(4):
            for which, (product, first_m, last_m) in enumerate(((vector, 0, 3), (tensor, 3, 8))):
                part = jnp.concatenate(
                    [product[128 * k + 32 * group : 128 * k + 32 * group + 32] for k in range(8)],
                    axis=0,
                )
                amp = jnp.dot(
                    spread[b, group, pl.ds(32 * first_m, 32 * (last_m - first_m)), :],
                    part,
                    preferred_element_type=F32,
                )
                norm = None
                for m in range(last_m - first_m):
                    piece = amp[32 * m : 32 * (m + 1)]
                    norm = piece * piece if norm is None else norm + piece * piece
                norms[which].append(norm.astype(BF16))
        joined = jnp.concatenate(
            [
                ext[1, 1 + hy, 1 + hz],
                scalar_part,
                jnp.concatenate(norms[0], axis=0),
                jnp.concatenate(norms[1], axis=0),
            ],
            axis=1,
        )
        mixed = jnp.dot(joined, mix_weight[...], preferred_element_type=F32)
        live_slot = lax.broadcasted_iota(jnp.int32, (128, 128), 0) < counts[0, hy, hz]
        out[0, hy, hz] = jnp.where(live_slot, mixed, 0.0).astype(BF16)

    def each_bin(body, hy=None):
        def step(b, carry):
            body(b if hy is None else 2 * hy + b)
            return carry

        lax.fori_loop(0, 4 if hy is None else 2, step, 0)

    def greet(barrier, device):
        pl.semaphore_signal(barrier, inc=1, device_id=device, device_id_type=MESH)

    half_y = size_y // 2
    upper = me_y // half_y
    in_half = lax.rem(me_y, half_y)
    at_edge = (in_half == 0) | (in_half == half_y - 1)
    first_far, second_far = at_edge & (upper == 0), at_edge & (upper == 1)
    idle_above = size_z - 1 - z_last

    def between(pair):
        low = pair < idle_above
        y_first = jnp.where(upper == 0, me_y, lax.rem(me_y + far_step + size_y, size_y))
        return (
            me_x,
            jnp.where(low, y_first, y_first + half_y),
            jnp.where(low, z_last + 1 + pair, pair - idle_above),
        )

    @pl.when(jnp.logical_not(live))
    def _():
        out[...] = jnp.zeros_like(out)
        low = (upper == 0) & (me_z > z_last)
        high = (upper == 1) & (me_z < z_first)

        @pl.when(at_edge & (low | high))
        def _():
            barrier = pltpu.get_barrier_semaphore()
            pair = jnp.where(low, me_z - z_last - 1, me_z + idle_above)
            pl.semaphore_wait(barrier, 2)
            pl.semaphore_signal(
                far_sem,
                inc=1,
                device_id=(me_x, me_y - half_y * upper, z_first + pair),
                device_id_type=MESH,
            )

    @pl.when(live)
    def _():
        barrier = pltpu.get_barrier_semaphore()
        pl.when(at_edge)(lambda: greet(barrier, between(me_z - z_first)))
        pl.when(jnp.logical_not(second_far))(lambda: greet(barrier, at(0, far_step, 0)))
        greet(barrier, at(0, -far_step, 0))
        for dx, dz in AROUND:
            pl.when(has(dz))(functools.partial(greet, barrier, at(dx, 0, dz)))

        inputs = [
            pltpu.make_async_copy(source, target, input_sem.at[n])
            for n, (source, target) in enumerate(
                (
                    (offs_in, offs),
                    (lists_in, lists),
                    (pairs_in, pairs),
                    (radial_in_in, radial_in),
                    (radial_out_in, radial_out),
                    (mix_weight_in, mix_weight),
                )
            )
        ]
        own_copy = pltpu.make_async_copy(feats.at[0], ext.at[1, pl.ds(1, 2), pl.ds(1, 2)], own_sem)
        own_copy.start()
        for copy in inputs:
            copy.start()
        inputs[0].wait()
        for y in range(2):
            for c in range(3):
                value = offs[0, y, c].astype(F32)
                for z in range(2):
                    places[1, 1, 1 + y, 3 * z + c : 3 * z + c + 1, :] = value[z : z + 1]
            places[1, 1, 1 + y, 6:8, :] = jnp.zeros((2, 128), F32)
        own_copy.wait()
        near = 3 + 3 * below.astype(jnp.int32) + 3 * above.astype(jnp.int32)
        pl.semaphore_wait(barrier, near + jnp.where(first_far, 0, 1))

        def send_far():
            place_y(late).start()
            feat_y(late).start()

        def greeted():
            pl.semaphore_wait(far_sem, 1)
            send_far()

        pl.when(jnp.logical_not(first_far))(send_far)
        place_y(early).start()
        feat_y(early).start()
        pl.when(jnp.logical_not(second_far))(lambda: start_around(feat_own()))

        @pl.when(jnp.logical_not(below))
        def _():
            ext[:, :, 0] = jnp.zeros((3, 4, 128, 128), BF16)

        @pl.when(jnp.logical_not(above))
        def _():
            ext[:, :, 3] = jnp.zeros((3, 4, 128, 128), BF16)

        for copy in inputs[1:]:
            copy.wait()
        each_bin(one_hots)

        @pl.when(second_far)
        def _():
            start_around(feat_own())

        place_y(1 - early).wait_recv()
        start_around(place_early())
        feat_y(1 - early).wait_recv()
        start_around(feat_early())
        recv_around(place_early())
        each_bin(geometry, early)
        recv_around(feat_own())
        each_bin(gather_inner)
        each_bin(gather_column, early)
        soon = me_z - z_first >= size_z // 4
        pl.when(first_far & soon)(greeted)
        recv_around(feat_early())
        each_bin(finish, early)
        pl.when(first_far & jnp.logical_not(soon))(greeted)
        place_y(early).wait_send()
        feat_y(early).wait_send()
        for copies in (place_early, feat_own, feat_early):
            send_around(copies())
        place_y(1 - late).wait_recv()
        start_around(place_late())
        feat_y(1 - late).wait_recv()
        start_around(feat_late())
        each_bin(gather_column, late)
        first_hz = jnp.where(above, 0, 1)

        def recv_from(copies, step, also):
            for (_, dz), copy in zip(AROUND, copies()):
                if dz == step:
                    pl.when(has(-dz) & also)(copy.wait_recv)

        def recv_first(copies):
            recv_from(copies, 0, live)
            recv_from(copies, 1, above)

        def recv_second(copies):
            recv_from(copies, 1, jnp.logical_not(above))
            recv_from(copies, -1, live)

        def last_bins(t, carry):
            b = 2 * late + jnp.where(t == 0, first_hz, 1 - first_hz)
            pl.when(t == 0)(lambda: recv_first(place_late))
            pl.when(t == 1)(lambda: recv_second(place_late))
            geometry(b)
            pl.when(t == 0)(lambda: recv_first(feat_late))

            @pl.when(t == 1)
            def _():
                place_y(late).wait_send()
                feat_y(late).wait_send()
                send_around(place_late())
                recv_second(feat_late)
                send_around(feat_late())

            finish(b)
            return carry

        lax.fori_loop(0, 2, last_bins, 0)


def per_device(sizes, *arrays):
    node_feats, offsets, counts, neighbours, pair_counts, radial_in, radial_out, mix_weight = arrays
    hbm = pl.BlockSpec(memory_space=pltpu.HBM)
    return pl.pallas_call(
        functools.partial(kernel, sizes),
        out_shape=pltpu.VMEM(node_feats.shape, BF16),
        in_specs=[hbm, hbm, hbm, hbm, pl.BlockSpec(memory_space=pltpu.SMEM), hbm, hbm, hbm],
        out_specs=pl.BlockSpec(memory_space=pltpu.VMEM),
        scratch_shapes=[
            pltpu.VMEM((1, 2, 3, 2, 128), BF16),
            pltpu.VMEM((1, 2, 2, 8, 128), jnp.int32),
            pltpu.VMEM((1, 2, 2, 128), jnp.int32),
            pltpu.VMEM((8, 64), F32),
            pltpu.VMEM((64, 384), BF16),
            pltpu.VMEM((512, 128), BF16),
            pltpu.VMEM((3, 4, 4, 128, 128), BF16),
            pltpu.VMEM((3, 3, 4, 8, 128), F32),
            pltpu.VMEM((4, 1024, 1152), BF16),
            pltpu.VMEM((4, 1024, 640), BF16),
            pltpu.VMEM((4, 128, 8), F32),
            pltpu.VMEM((4, 4, 256, 256), BF16),
            pltpu.VMEM((4, 1024, 384), BF16),
            pltpu.VMEM((4, 1024, 128), F32),
            pltpu.SemaphoreType.DMA,
            pltpu.SemaphoreType.DMA((6,)),
            pltpu.SemaphoreType.DMA((44,)),
            pltpu.SemaphoreType.DMA((44,)),
            pltpu.SemaphoreType.REGULAR,
        ],
        compiler_params=pltpu.CompilerParams(
            collective_id=0, has_side_effects=True, vmem_limit_bytes=65344 * 1024
        ),
        cost_estimate=pl.CostEstimate(
            flops=4_000_000_000, bytes_accessed=4_000_000, transcendentals=600_000
        ),
    )(
        node_feats,
        jnp.transpose(offsets, (0, 1, 3, 2, 4)),
        jnp.swapaxes(neighbours, 3, 4),
        pair_counts,
        counts,
        radial_in,
        radial_out,
        mix_weight,
    )


def solution(mesh):
    placed = (
        P("gx", "gy", "gz", None, None),
        P("gx", "gy", "gz", None, None),
        P("gx", "gy", "gz"),
        P("gx", "gy", "gz", None, None),
        P("gx", "gy", "gz", None),
        P(),
        P(),
        P(),
    )
    sizes = tuple(mesh.shape[axis] for axis in AXES)
    return jax.shard_map(
        functools.partial(per_device, sizes),
        mesh=mesh,
        in_specs=placed,
        out_specs=P("gx", "gy", "gz", None, None),
        check_vma=False,
    )
```
